256 devices in a mesh: rows: 32 (over z, y), dim: 8 (over x, core).
Axes of the slice: x: 4, y: 4, z: 8, core: 2. Of those that a mesh axis runs over, the one named last changes fastest.
Arguments:
- embeddings: bfloat16 [294912, 4096], P('rows', 'dim'), may hold values from -1 to 1
- quality: float32 [294912], P(('rows', 'dim')), may hold values from 0.5 to 4
- picked_rows: int32 [3, 64], replicated, may hold values from 0 to 294911, as said below
Outputs:
- factor_rows: float32 [294912, 192], P(('rows', 'dim'))
- residual_diag: float32 [294912], P(('rows', 'dim'))
The draws below stay inside these ranges and needn't reach their ends.
Inputs may be any that keep to these rules, and one draw needn't show every extreme that they name: `picked_rows`: all 192 indices are different.
All inputs are finite; a program needn't handle non-finite values.
Results may differ from the reference program's by a relative error of at most 0.0003.
Values may be sent and summed in bfloat16 or wider, within the bound.
No kernel may reach another device: no remote copies, remote signals or barrier semaphores. Data moves between devices by JAX's collectives and lax.ppermute only.
A program may use at most 128 MiB of HBM per device.

```python
import math
import jax
import jax.numpy as jnp
from jax import lax

D = 4096
ROWS_DEV = 9216
PICKS = 64
ROUNDS = 3
RANK = 192
POOL = 294912


cluster_count = 16


def draw_embeddings(key, part):
    key = jax.random.fold_in(key, 5)
    mean_key, centre_key, block_key = jax.random.split(key, 3)
    spread = D ** (-0.5)
    common = jnp.clip(jax.random.normal(mean_key, (D,), jnp.float32), -4.0, 4.0)
    centres = jnp.clip(jax.random.normal(centre_key, (cluster_count, D), jnp.float32), -4.0, 4.0)
    weights = (0.4, 0.5, 0.77)

    def one_block(index):
        local = jax.random.fold_in(block_key, index)
        label_key, noise_key = jax.random.split(local, 2)
        labels = jax.random.randint(label_key, (ROWS_DEV,), 0, cluster_count)
        noise = jnp.clip(jax.random.normal(noise_key, (ROWS_DEV, D), jnp.float32), -4.0, 4.0)
        row_scale = jnp.ones((ROWS_DEV, 1), jnp.float32)
        mixed = weights[0] * common[None, :] + weights[1] * centres[labels] + weights[2] * noise
        return (mixed * (row_scale * spread)).astype(jnp.bfloat16)
    blocks = lax.map(one_block, jnp.arange(POOL // ROWS_DEV, dtype=jnp.int32))
    return blocks.reshape(POOL, D)


def draw_picked_rows(key, part):
    key = jax.random.fold_in(key, 11)
    first_key, second_key, label_key, local_key = jax.random.split(key, 4)
    owners = POOL // ROWS_DEV
    total = ROUNDS * PICKS
    first = jax.random.randint(first_key, (total,), 0, owners)
    second = jax.random.randint(second_key, (total,), 0, owners)
    ranked = jnp.minimum(first, second)
    relabel = jax.random.permutation(label_key, owners)
    owner_index = relabel[ranked]
    local_index = jax.random.permutation(local_key, ROWS_DEV)[:total]
    return (owner_index * ROWS_DEV + local_index).reshape(ROUNDS, PICKS).astype(jnp.int32)


def block_levels(key, shape, cuts, smallest, largest):
    def one(position, blocks):
        heights = jax.random.uniform(jax.random.fold_in(jax.random.fold_in(key, 6), position), (blocks,), jnp.float32, smallest / len(cuts), largest / len(cuts))
        return jnp.repeat(jnp.exp(heights), shape[position] // blocks).reshape((-1,) + (1,) * (len(shape) - position - 1))

    factor_of = one(*cuts[0])
    for cut in cuts[1:]:
        factor_of = factor_of * one(*cut)
    return factor_of


def setup_inputs(seed: int = 0) -> dict:
    seeds = jax.random.split(jax.random.key(seed), 4)
    embeddings = draw_embeddings(jax.random.fold_in(seeds[3], 71), 0)
    quality = jnp.clip(jnp.exp(math.log(4.0) - 2.0794415 * jax.random.uniform(seeds[1], (POOL,), jnp.float32) ** block_levels(seeds[1], (POOL,), ((0, 256),), -0.2, 0.2)), 0.5, 4.0)
    picked_rows = draw_picked_rows(jax.random.fold_in(seeds[3], 71), 0)
    return dict(embeddings=embeddings, quality=quality, picked_rows=picked_rows)


ridge_term = 0.5

def reference(embeddings, quality, picked_rows):
    blocks = embeddings.reshape(POOL // ROWS_DEV, ROWS_DEV, D)
    norms = lax.map(lambda block: jnp.einsum('rd,rd->r', block.astype(jnp.float32), block.astype(jnp.float32), preferred_element_type=jnp.float32), blocks).reshape(POOL)
    residual_diag = quality * quality * (norms + ridge_term)
    factor_rows = jnp.zeros((POOL, RANK), jnp.float32)
    row_global = jnp.arange(POOL, dtype=jnp.int32)
    eye_block = jnp.eye(PICKS, dtype=jnp.float32)
    for counter in range(ROUNDS):
        chosen = picked_rows[counter]
        pick_emb = embeddings[chosen]
        pick_quality = quality[chosen]
        pick_factor = factor_rows[chosen]
        kernel_rows = lax.map(lambda block: jnp.einsum('rd,pd->rp', block.astype(jnp.float32), pick_emb.astype(jnp.float32), preferred_element_type=jnp.float32), blocks).reshape(POOL, PICKS)
        kernel_rows = kernel_rows + ridge_term * (row_global[:, None] == chosen[None, :]).astype(jnp.float32)
        schur = quality[:, None] * pick_quality[None, :] * kernel_rows - jnp.dot(factor_rows, pick_factor.T, precision=lax.Precision.HIGHEST)
        pick_gram = jnp.einsum('pd,qd->pq', pick_emb.astype(jnp.float32), pick_emb.astype(jnp.float32), preferred_element_type=jnp.float32) + ridge_term * eye_block
        pick_kernel = pick_quality[:, None] * pick_quality[None, :] * pick_gram - jnp.dot(pick_factor, pick_factor.T, precision=lax.Precision.HIGHEST)
        lower_factor = jnp.linalg.cholesky(pick_kernel)
        new_columns = jax.scipy.linalg.solve_triangular(lower_factor, schur.T, lower=True).T
        factor_rows = factor_rows.at[:, counter * PICKS:(counter + 1) * PICKS].set(new_columns)
        residual_diag = residual_diag - jnp.sum(new_columns * new_columns, axis=1)
    return (factor_rows, residual_diag)
```

```python
import functools

import jax
import jax.numpy as jnp
from jax import lax
from jax.experimental import pallas as pl
from jax.experimental.pallas import tpu as pltpu
from jax.sharding import PartitionSpec as P

ridge_term = 0.5
pack = 1152
Y, Z, X = 4, 8, 4
HIGHEST = lax.Precision.HIGHEST
NT = (((1,), (1,)), ((), ()))
TN = (((0,), (0,)), ((), ()))
f32, bf16, i32, i16 = jnp.float32, jnp.bfloat16, jnp.int32, jnp.int16
VMEM = pl.BlockSpec(memory_space=pltpu.VMEM)
levels = 32767.0


def params(mib):
    return pltpu.CompilerParams(vmem_limit_bytes=mib << 20)


def cost(flops, nbytes):
    return pl.CostEstimate(flops=int(flops), bytes_accessed=int(nbytes), transcendentals=0)


def shape(dims, dtype):
    return jax.ShapeDtypeStruct(dims, dtype)


def as_column(row):
    n = row.shape[1]
    eye = lax.broadcasted_iota(i32, (n, n), 0) == lax.broadcasted_iota(i32, (n, n), 1)
    wide = jnp.broadcast_to(row.astype(f32), (n, n))
    return jnp.sum(jnp.where(eye, wide, 0.0), axis=1, keepdims=True).astype(i32)


def pick_kernel(picks_ref, e_ref, *rest):
    outs, (idx_ref, acc_ref) = rest[:Y], rest[Y:]
    step = pl.program_id(0)
    tile = e_ref.shape[0]
    rounds, count = picks_ref.shape
    total = rounds * count
    row_start = lax.axis_index("rows") * (tile * pl.num_programs(0))

    @pl.when(step == 0)
    def _():
        for r in range(rounds):
            column = as_column(picks_ref[r : r + 1, :]) - row_start
            idx_ref[r * count : (r + 1) * count, :] = jnp.broadcast_to(column, (count, 128))
        acc_ref[...] = jnp.zeros_like(acc_ref)

    here = idx_ref[...] - step * tile
    lane = lax.broadcasted_iota(i32, (total, 128), 1)
    hot = jnp.concatenate(
        [jnp.where(here == lane + 128 * j, 1.0, 0.0).astype(bf16) for j in range(tile // 128)], axis=1
    )
    acc_ref[...] += jnp.dot(hot, e_ref[...], preferred_element_type=f32)

    @pl.when(step == pl.num_programs(0) - 1)
    def _():
        y = lax.rem(lax.axis_index("rows"), Y)
        group = total // Y
        for j in range(Y):
            g = lax.rem(y + j, Y)
            outs[j][...] = acc_ref[pl.ds(pl.multiple_of(g * group, 16), group), :].astype(bf16)


def local_picks(picks, embeddings):
    rows, dims = embeddings.shape
    total = picks.size
    tile = 1024
    return pl.pallas_call(
        pick_kernel,
        grid=(rows // tile,),
        in_specs=[VMEM, pl.BlockSpec((tile, dims), lambda i: (i, 0))],
        out_specs=[pl.BlockSpec((total // Y, dims), lambda i: (0, 0))] * Y,
        out_shape=[shape((total // Y, dims), bf16)] * Y,
        scratch_shapes=[pltpu.VMEM((total, 128), i32), pltpu.VMEM((total, dims), f32)],
        compiler_params=params(48),
        cost_estimate=cost(2 * rows * dims * total, rows * dims * 2),
        name="local_picks",
    )(picks, embeddings)


def gram_kernel(s0, s1, s2, s3, mine_ref, other_ref, gram_ref):
    y = lax.rem(lax.axis_index("rows"), Y)
    group = s0.shape[0] // 2
    for j, ref in enumerate((s0, s1, s2, s3)):
        g = pl.multiple_of(lax.rem(y + (Y - j), Y) * group, 16)
        mine_ref[pl.ds(g, group), :] = ref[:group, :]
        other_ref[pl.ds(g, group), :] = ref[group:, :]
    mine, other = mine_ref[...], other_ref[...]
    gram = lax.dot_general(mine, mine, NT, preferred_element_type=f32)
    gram += lax.dot_general(other, other, NT, preferred_element_type=f32)
    core = lax.rem(lax.axis_index("dim"), 2)

    @pl.when(core == 0)
    def _():
        gram_ref[...] = gram[:128, :128]

    @pl.when(core == 1)
    def _():
        gram_ref[...] = jnp.zeros_like(gram_ref)
        gram_ref[:64, :] = gram[128:, :128]
        gram_ref[64:, :64] = gram[128:, 128:]


def picks_and_gram(parts):
    both, dims = parts[0].shape
    total = both // 2 * Y
    return pl.pallas_call(
        gram_kernel,
        in_specs=[VMEM] * Y,
        out_specs=[VMEM] * 3,
        out_shape=[shape((total, dims), bf16), shape((total, dims), bf16), shape((128, 128), f32)],
        compiler_params=params(16),
        cost_estimate=cost(4 * total * total * dims, 4 * total * dims),
        name="gram",
    )(*parts)


panel = 32


def factor_kernel(mine_ref, other_ref, inverse_ref, m_ref):
    n = inverse_ref.shape[0]
    core = lax.rem(lax.axis_index("dim"), 2)
    first = jnp.where(core == 0, mine_ref[...], other_ref[...])
    last = jnp.where(core == 0, other_ref[...], mine_ref[...])
    width = m_ref.shape[1]
    sub = lax.broadcasted_iota(i32, (n, width - 128), 0)
    lane = lax.broadcasted_iota(i32, (n, width - 128), 1) + 128
    m_ref[:, 128:] = jnp.where(lane - n == sub, 1.0, 0.0)
    diag = lax.broadcasted_iota(i32, (128, 128), 0) == lax.broadcasted_iota(i32, (128, 128), 1)
    ridge = jnp.where(diag, ridge_term, 0.0)
    m_ref[:128, :128] = first + ridge
    m_ref[128:, :128] = last[:64, :]
    m_ref[128:, 128:n] = last[64:, :64] + ridge[:64, :64]
    m_ref[:128, 128:n] = last[:64, :].T
    below = lax.broadcasted_iota(i32, (panel, 1), 0)
    at = lax.broadcasted_iota(i32, (panel, width), 1) - lax.broadcasted_iota(i32, (panel, width), 0)
    for low in range(0, n, panel):
        rows = m_ref[low : low + panel, :]
        for t in range(0, panel, 2):
            c1, c2 = rows[:, low + t : low + t + 1], rows[:, low + t + 1 : low + t + 2]
            r1, r2 = rows[t : t + 1, :], rows[t + 1 : t + 2, :]
            a, b, d = c1[t : t + 1], c2[t : t + 1], c2[t + 1 : t + 2]
            over_a = 1.0 / a
            l = b * over_a
            over_d = 1.0 / (d - l * b)
            m1 = jnp.where(below > t, c1 * over_a, 0.0)
            m2 = jnp.where(below > t + 1, (c2 - l * c1) * over_d, 0.0)
            rows = rows - m1 * r1 - m2 * (r2 - l * r1)
        pivots = jnp.sum(jnp.where(at == low, rows, 0.0), axis=1, keepdims=True)
        rows = rows * (1.0 / jnp.sqrt(pivots))
        inverse_ref[low : low + panel, :] = rows[:, n:]
        if low + panel < n:
            update = lax.dot_general(rows[:, :n], rows, TN, precision=HIGHEST, preferred_element_type=f32)
            m_ref[low + panel :, :] -= update[low + panel :, :]


def factor_inverse(mine, other, n):
    return pl.pallas_call(
        factor_kernel,
        in_specs=[VMEM] * 2,
        out_specs=VMEM,
        out_shape=shape((n, n), f32),
        scratch_shapes=[pltpu.VMEM((n, 2 * n), f32)],
        compiler_params=params(16),
        cost_estimate=cost(1e10, 1 << 20),
        name="factor",
    )(mine, other)


def block_products(e_ref, r_ref, mine_ref, other_ref):
    e, r = e_ref[...], r_ref[...]
    part = lax.dot_general(mine_ref[...], e, NT, preferred_element_type=f32)
    part += lax.dot_general(other_ref[...], r, NT, preferred_element_type=f32)
    squares = jnp.zeros((e.shape[0], 128), f32)
    for j in range(0, e.shape[1], 128):
        ej, rj = e[:, j : j + 128].astype(f32), r[:, j : j + 128].astype(f32)
        squares += ej * ej + rj * rj
    norm = lax.dot_general(jnp.ones((8, 128), f32), squares, NT, precision=HIGHEST, preferred_element_type=f32)
    return part, norm


def split(value):
    scaled = value * 16.0
    high = jnp.floor(scaled)
    return high, jnp.floor((scaled - high) * 32768.0)


def join(high, low):
    return (high + low * (1.0 / 32768.0)) * (1.0 / 16.0)


def send_kernel(place_ref, e_ref, r_ref, mine_ref, other_ref, out_ref):
    part, norm = block_products(e_ref, r_ref, mine_ref, other_ref)
    norm_high, norm_low = split(norm[:1])
    top_high, top_low = split(jnp.max(jnp.abs(part), axis=0, keepdims=True))
    scale = join(top_high, top_low + 1.0)
    coded = jnp.floor(part * (levels / scale) + 0.5)
    row = lax.broadcasted_iota(i32, (8, part.shape[1]), 0)
    extra = jnp.where(row == 0, norm_high, jnp.where(row == 1, norm_low, jnp.where(row == 2, top_high, top_low)))
    out_ref[...] = jnp.concatenate([coded, extra], axis=0).astype(i32).astype(i16)


def keep_kernel(place_ref, e_ref, r_ref, mine_ref, other_ref, out_ref, norm_ref):
    part, norm = block_products(e_ref, r_ref, mine_ref, other_ref)
    out_ref[...] = part
    norm_ref[...] = norm


def products(hop, place, embeddings, received, mine, other, tile=384):
    total, dims = mine.shape
    steps = pack // tile

    def own(i, place):
        return (lax.rem(place[0] + hop, X) * 2 + place[1]) * steps + i, 0

    def got(i, place):
        return lax.rem(place[0] + hop, X) * steps + i, 0

    def fixed(i, place):
        return 0, 0

    def along(i, place):
        return 0, i

    send = hop > 0
    out_shape = [shape((total + 8, pack), i16)] if send else [shape((total, pack), f32), shape((8, pack), f32)]
    return pl.pallas_call(
        send_kernel if send else keep_kernel,
        grid_spec=pltpu.PrefetchScalarGridSpec(
            num_scalar_prefetch=1,
            grid=(steps,),
            in_specs=[
                pl.BlockSpec((tile, dims), own),
                pl.BlockSpec((tile, dims), got),
                pl.BlockSpec((total, dims), fixed),
                pl.BlockSpec((total, dims), fixed),
            ],
            out_specs=[pl.BlockSpec((s.shape[0], tile), along) for s in out_shape],
        ),
        out_shape=out_shape,
        compiler_params=params(32),
        cost_estimate=cost(4 * pack * dims * total, 4 * pack * dims),
        name="products_%d" % hop,
    )(place, embeddings, received, mine, other)


def finish_kernel(picks_ref, quality_ref, own_ref, norm_ref, g1, g2, g3, inverse_ref, out_ref, resid_ref):
    total, width = own_ref.shape
    rounds, count = picks_ref.shape
    first_row = (lax.axis_index("rows") * (2 * X) + lax.axis_index("dim")) * width
    chosen = jnp.concatenate([as_column(picks_ref[r : r + 1, :]) for r in range(rounds)], axis=0) - first_row
    inverse = inverse_ref[...]
    tile = 384
    for low in range(0, width, tile):
        here = pl.ds(low, tile)
        values, norm = own_ref[:, here], norm_ref[:1, here]
        for ref in (g1, g2, g3):
            got = ref[:, here].astype(i32).astype(f32)
            scale = join(got[total + 2 : total + 3], got[total + 3 : total + 4] + 1.0)
            values = values + got[:total] * (scale * (1.0 / levels))
            norm = norm + join(got[total : total + 1], got[total + 1 : total + 2] + 0.5)
        lane = lax.broadcasted_iota(i32, (total, tile), 1) + low
        values = jnp.where(chosen == lane, values + ridge_term, values)
        columns = jnp.dot(inverse, values, precision=HIGHEST, preferred_element_type=f32)
        score = quality_ref[here].reshape(1, tile)
        out_ref[:, here] = columns * score
        left = norm + ridge_term - jnp.sum(columns * columns, axis=0, keepdims=True)
        resid_ref[here] = (score * score * left).reshape(tile)


def finish(picks, quality, own, norm, got, inverse):
    total, width = own.shape
    return pl.pallas_call(
        finish_kernel,
        in_specs=[VMEM] * 8,
        out_specs=[VMEM] * 2,
        out_shape=[shape((total, width), f32), shape((width,), f32)],
        compiler_params=params(32),
        cost_estimate=cost(12 * total * total * width, 4 << 20),
        name="finish",
    )(picks, quality, own, norm, *got, inverse)


def along_y(k):
    return [(r, r // Y * Y + (r % Y + k) % Y) for r in range(Y * Z)]


def along_z(k):
    return [(r, (r // Y + k) % Z * Y + r % Y) for r in range(Y * Z)]


def along_x(k):
    return [(d, (d // 2 + k) % X * 2 + d % 2) for d in range(2 * X)]


def both_ways_z(k):
    pairs = []
    for r in range(Y * Z):
        for d in range(2 * X):
            z = (r // Y + (k if d % 2 == 0 else -k)) % Z
            pairs.append((r * 2 * X + d, (z * Y + r % Y) * 2 * X + d))
    return pairs


swap = [(d, d ^ 1) for d in range(2 * X)]


def per_device(embeddings, quality, picked_rows):
    rows_here, dims_here = embeddings.shape
    total = picked_rows.size
    group = total // Y
    d = lax.axis_index("dim")
    place = jnp.stack([d // 2, d % 2]).astype(i32)

    with jax.named_scope("swap_rows"):
        halves = embeddings.reshape(X, 2, pack, dims_here)
        away = lax.dynamic_index_in_dim(halves, 1 - d % 2, 1, keepdims=False)
        received = lax.ppermute(away.reshape(X * pack, dims_here), "dim", swap)

    with jax.named_scope("gather_picks"):
        parts = local_picks(picked_rows, embeddings)
        mine = parts[0]
        for k in range(1, Y):
            mine = mine + lax.ppermute(parts[k], "rows", along_y(k))
        both = jnp.concatenate([mine, lax.ppermute(mine, "dim", swap)], axis=0)
        arrived = [lax.ppermute(both, ("rows", "dim"), both_ways_z(k)) for k in (1, 2, 3)]
        far = lax.ppermute(mine, "rows", along_z(4))
        near = arrived[0] + arrived[1] + arrived[2]
        partial = jnp.concatenate([near[:group] + mine + far, near[group:]], axis=0)
        turned = lax.ppermute(partial, "dim", swap)
        full = partial + jnp.concatenate([turned[group:], turned[:group]], axis=0)
        groups = [full] + [lax.ppermute(full, "rows", along_y(k)) for k in range(1, Y)]

    pick_mine, pick_other, gram = picks_and_gram(groups)
    with jax.named_scope("sum_gram"):
        for_sum = [lax.ppermute(gram, "dim", along_x(k)) for k in (1, 2, 3)]
        gram = gram + for_sum[0] + for_sum[1] + for_sum[2]
        gram_other = lax.ppermute(gram, "dim", swap)

    got = []
    for hop in (2, 1, 3):
        coded = products(hop, place, embeddings, received, pick_mine, pick_other)[0]
        got.append(lax.ppermute(coded, "dim", along_x(hop)))
    own, norm = products(0, place, embeddings, received, pick_mine, pick_other)
    inverse = factor_inverse(gram, gram_other, total)
    columns, residual = finish(picked_rows, quality, own, norm, got, inverse)
    return columns.T, residual


def solution(mesh):
    return jax.shard_map(
        per_device,
        mesh=mesh,
        in_specs=(P("rows", "dim"), P(("rows", "dim")), P()),
        out_specs=(P(("rows", "dim"), None), P(("rows", "dim"))),
        check_vma=False,
    )
```

```python
import functools

import jax
import jax.numpy as jnp
from jax import lax
from jax.experimental import pallas as pl
from jax.experimental.pallas import tpu as pltpu
from jax.sharding import PartitionSpec as P

ridge_term = 0.5
pack = 1152
Y, Z, X = 4, 8, 4
HIGHEST = lax.Precision.HIGHEST
NT = (((1,), (1,)), ((), ()))
TN = (((0,), (0,)), ((), ()))
f32, bf16, i32, i16 = jnp.float32, jnp.bfloat16, jnp.int32, jnp.int16
VMEM = pl.BlockSpec(memory_space=pltpu.VMEM)
ANY = pl.BlockSpec(memory_space=pl.ANY)
levels = 32767.0


def params(mib):
    return pltpu.CompilerParams(vmem_limit_bytes=mib << 20)


def cost(flops, nbytes):
    return pl.CostEstimate(flops=int(flops), bytes_accessed=int(nbytes), transcendentals=0)


def shape(dims, dtype):
    return jax.ShapeDtypeStruct(dims, dtype)


def as_column(row):
    n = row.shape[1]
    eye = lax.broadcasted_iota(i32, (n, n), 0) == lax.broadcasted_iota(i32, (n, n), 1)
    wide = jnp.broadcast_to(row.astype(f32), (n, n))
    return jnp.sum(jnp.where(eye, wide, 0.0), axis=1, keepdims=True).astype(i32)


def pick_kernel(picks_ref, e_ref, *rest):
    outs, (list_ref, tiles_ref, rows_ref, arrived) = rest[:Y], rest[Y:]
    rounds, count = picks_ref.shape
    total = rounds * count
    height = tiles_ref.shape[1]
    rows_here = e_ref.shape[0]
    row_start = lax.axis_index("rows") * rows_here
    held = jnp.int32(0)
    for p in range(total):
        local = picks_ref[p // count, p % count] - row_start
        list_ref[held] = local * 256 + p
        held = held + jnp.where((local >= 0) & (local < rows_here), 1, 0)

    def fetch(i):
        tile = pl.multiple_of(lax.div(list_ref[i], 256 * height) * height, height)
        return pltpu.make_async_copy(e_ref.at[pl.ds(tile, height), :], tiles_ref.at[i], arrived.at[i])

    def begin(i, carry):
        fetch(i).start()
        return carry

    def end(i, carry):
        fetch(i).wait()
        sub = lax.broadcasted_iota(i32, tiles_ref.shape[1:], 0)
        place, p = lax.div(list_ref[i], 256), lax.rem(list_ref[i], 256)
        one = jnp.where(sub == lax.rem(place, height), tiles_ref[i].astype(f32), 0.0)
        rows_ref[pl.ds(p, 1), :] = jnp.sum(one, axis=0, keepdims=True)
        return carry

    lax.fori_loop(0, held, begin, 0)
    rows_ref[...] = jnp.zeros_like(rows_ref)
    lax.fori_loop(0, held, end, 0)
    y = lax.rem(lax.axis_index("rows"), Y)
    group = total // Y
    for j in range(Y):
        g = lax.rem(y + j, Y)
        outs[j][...] = rows_ref[pl.ds(pl.multiple_of(g * group, 16), group), :].astype(bf16)


def local_picks(picks, embeddings):
    dims = embeddings.shape[1]
    total = picks.size
    return pl.pallas_call(
        pick_kernel,
        in_specs=[pl.BlockSpec(memory_space=pltpu.SMEM), ANY],
        out_specs=[VMEM] * Y,
        out_shape=[shape((total // Y, dims), bf16)] * Y,
        scratch_shapes=[
            pltpu.SMEM((256,), i32),
            pltpu.VMEM((total, 16, dims), bf16),
            pltpu.VMEM((total, dims), f32),
            pltpu.SemaphoreType.DMA((total,)),
        ],
        compiler_params=params(50),
        cost_estimate=cost(0, 10 << 20),
        name="local_picks",
    )(picks, embeddings)


def stage_kernel(hop, e_ref, r_ref, through_ref, mine_ref, other_ref, norm_ref, passed_ref, arrived):
    d = lax.axis_index("dim")
    chip, core = lax.div(d, 2), lax.rem(d, 2)
    first = (lax.rem(chip + hop, X) * 2 + core) * pack
    tile = pack // 3
    copies = []
    for i in range(3):
        there, here = pl.ds(pl.multiple_of(first + i * tile, 128), tile), pl.ds(i * tile, tile)
        copies.append(
            (
                pltpu.make_async_copy(e_ref.at[there, :], mine_ref.at[here, :], arrived.at[2 * i]),
                pltpu.make_async_copy(r_ref.at[there, :], other_ref.at[here, :], arrived.at[2 * i + 1]),
            )
        )
    for pair in copies:
        for copy in pair:
            copy.start()
    passed_ref[...] = through_ref[...]
    for i in range(3):
        for copy in copies[i]:
            copy.wait()
        squares = jnp.zeros((tile, 128), f32)
        for ref in (mine_ref, other_ref):
            for j in range(0, ref.shape[1], 128):
                part = ref[i * tile : (i + 1) * tile, j : j + 128].astype(f32)
                squares += part * part
        high = squares.astype(bf16)
        low = (squares - high.astype(f32)).astype(bf16)
        ones = jnp.ones((8, 128), bf16)
        norm = lax.dot_general(ones, high, NT, preferred_element_type=f32)
        norm_ref[:, i * tile : (i + 1) * tile] = norm + lax.dot_general(ones, low, NT, preferred_element_type=f32)


def stage(hop, embeddings, received, through):
    dims = embeddings.shape[1]
    return pl.pallas_call(
        functools.partial(stage_kernel, hop),
        in_specs=[ANY, ANY, VMEM],
        out_specs=[VMEM] * 4,
        out_shape=[
            shape((pack, dims), bf16),
            shape((pack, dims), bf16),
            shape((8, pack), f32),
            shape(through.shape, through.dtype),
        ],
        scratch_shapes=[pltpu.SemaphoreType.DMA((6,))],
        compiler_params=params(52),
        cost_estimate=cost(0, 4 * pack * dims),
        name="stage_%d" % hop,
    )(embeddings, received, through)


def order_kernel(s0, s1, s2, s3, out_ref):
    y = lax.rem(lax.axis_index("rows"), Y)
    group = s0.shape[0]
    for j, ref in enumerate((s0, s1, s2, s3)):
        g = pl.multiple_of(lax.rem(y + (Y - j), Y) * group, 16)
        out_ref[pl.ds(g, group), :] = ref[...]


def in_order(groups):
    group, dims = groups[0].shape
    return pl.pallas_call(
        order_kernel,
        in_specs=[VMEM] * Y,
        out_specs=VMEM,
        out_shape=shape((group * Y, dims), bf16),
        compiler_params=params(16),
        cost_estimate=cost(0, 4 * Y * group * dims),
        name="order",
    )(*groups)


def gram_kernel(mine_ref, other_ref, full_ref, half_ref, keep_ref):
    mine, other = mine_ref[...], other_ref[...]
    gram = lax.dot_general(mine, mine, NT, preferred_element_type=f32)
    gram += lax.dot_general(other, other, NT, preferred_element_type=f32)
    core = lax.rem(lax.axis_index("dim"), 2)
    top = gram[:128, :128]
    corner = jnp.concatenate([gram[128:, 128:], jnp.zeros((64, 64), f32)], axis=1)
    low = jnp.concatenate([gram[128:, :128], corner], axis=0)
    a, b = jnp.where(core == 0, top, low), jnp.where(core == 0, low, top)
    half_ref[...] = a
    full_ref[:128, :], full_ref[128:, :] = a, b
    keep_ref[:128, :], keep_ref[128:, :] = jnp.where(core == 0, a, 0.0), jnp.where(core == 0, b, 0.0)


def picks_gram(mine, other):
    total, dims = mine.shape
    return pl.pallas_call(
        gram_kernel,
        in_specs=[VMEM] * 2,
        out_specs=[VMEM] * 3,
        out_shape=[shape((256, 128), f32), shape((128, 128), f32), shape((256, 128), f32)],
        compiler_params=params(16),
        cost_estimate=cost(4 * total * total * dims, 4 * total * dims),
        name="gram",
    )(mine, other)


panel, together = 64, 8


def factor_kernel(sum_ref, swapped_ref, inverse_ref, m_ref):
    n = inverse_ref.shape[0]
    core = lax.rem(lax.axis_index("dim"), 2)
    a = sum_ref[:128, :] + swapped_ref[128:, :]
    b = sum_ref[128:, :] + swapped_ref[:128, :]
    first, last = jnp.where(core == 0, a, b), jnp.where(core == 0, b, a)
    width = m_ref.shape[1]
    sub = lax.broadcasted_iota(i32, (n, width - 128), 0)
    lane = lax.broadcasted_iota(i32, (n, width - 128), 1) + 128
    m_ref[:, 128:] = jnp.where(lane - n == sub, 1.0, 0.0)
    diag = lax.broadcasted_iota(i32, (128, 128), 0) == lax.broadcasted_iota(i32, (128, 128), 1)
    ridge = jnp.where(diag, ridge_term, 0.0)
    m_ref[:128, :128] = first + ridge
    m_ref[128:, :128] = last[:64, :]
    m_ref[128:, 128:n] = last[64:, :64] + ridge[:64, :64]
    m_ref[:128, 128:n] = last[:64, :].T
    below = lax.broadcasted_iota(i32, (panel, 128), 0)
    at = lax.broadcasted_iota(i32, (panel, 128), 1) - below
    for low in range(0, n, panel):
        left = low // 128 * 128
        off = low - left
        tiles = [m_ref[low : low + panel, j : j + 128] for j in range(left, width, 128)]
        for g in range(0, panel, together):
            cols = [
                jnp.broadcast_to(tiles[0][:, off + g + i : off + g + i + 1], (panel, 128)) for i in range(together)
            ]
            heads = [[t[g + i : g + i + 1, :] for t in tiles] for i in range(together)]
            for i in range(together):
                factors = jnp.where(below > g + i, cols[i] * (1.0 / cols[i][g + i : g + i + 1, :]), 0.0)
                for j in range(i + 1, together):
                    cols[j] = cols[j] - factors * cols[j][g + i : g + i + 1, :]
                    by = factors[g + j : g + j + 1, :]
                    heads[j] = [x - by * y for x, y in zip(heads[j], heads[i])]
                tiles = [t - factors * y for t, y in zip(tiles, heads[i])]
        pivots = jnp.sum(jnp.where(at == off, tiles[0], 0.0), axis=1, keepdims=True)
        rows = jnp.concatenate(tiles, axis=1) * (1.0 / jnp.sqrt(pivots))
        inverse_ref[low : low + panel, :] = rows[:, n - left :]
        if low + panel < n:
            update = lax.dot_general(rows[:, : n - left], rows, TN, precision=HIGHEST, preferred_element_type=f32)
            m_ref[low + panel :, left:] -= update[low + panel - left :, :]


def factor_inverse(total, swapped, n):
    return pl.pallas_call(
        factor_kernel,
        in_specs=[VMEM] * 2,
        out_specs=VMEM,
        out_shape=shape((n, n), f32),
        scratch_shapes=[pltpu.VMEM((n, 2 * n), f32)],
        compiler_params=params(16),
        cost_estimate=cost(1e6, 1 << 16),
        name="factor",
    )(total, swapped)


def split(value):
    scaled = value * 16.0
    high = jnp.floor(scaled)
    return high, jnp.floor((scaled - high) * 32768.0)


def join(high, low):
    return (high + low * (1.0 / 32768.0)) * (1.0 / 16.0)


def block_products(at, e_ref, r_ref, mine_ref, other_ref):
    part = lax.dot_general(mine_ref[...], e_ref[at, :], NT, preferred_element_type=f32)
    return part + lax.dot_general(other_ref[...], r_ref[at, :], NT, preferred_element_type=f32)


def send_kernel(e_ref, r_ref, norm_ref, mine_ref, other_ref, through_ref, out_ref, passed_ref):
    tile = pack // 3
    passed_ref[...] = through_ref[...]
    for low in range(0, pack, tile):
        at = pl.ds(low, tile)
        part = block_products(at, e_ref, r_ref, mine_ref, other_ref)
        norm_high, norm_low = split(norm_ref[:1, at])
        top_high, top_low = split(jnp.max(jnp.abs(part), axis=0, keepdims=True))
        scale = join(top_high, top_low + 1.0)
        coded = jnp.floor(part * (levels / scale) + 0.5)
        row = lax.broadcasted_iota(i32, (8, tile), 0)
        extra = jnp.where(row == 0, norm_high, jnp.where(row == 1, norm_low, jnp.where(row == 2, top_high, top_low)))
        out_ref[:, at] = jnp.concatenate([coded, extra], axis=0).astype(i32).astype(i16)


def keep_kernel(e_ref, r_ref, mine_ref, other_ref, out_ref):
    tile = pack // 3
    for low in range(0, pack, tile):
        out_ref[:, low : low + tile] = block_products(pl.ds(low, tile), e_ref, r_ref, mine_ref, other_ref)


def products(hop, staged, mine, other, through=None):
    total, dims = mine.shape
    if hop:
        operands = (*staged, mine, other, through)
        out_shape = [shape((total + 8, pack), i16), shape(through.shape, through.dtype)]
    else:
        operands = (*staged[:2], mine, other)
        out_shape = [shape((total, pack), f32)]
    return pl.pallas_call(
        send_kernel if hop else keep_kernel,
        in_specs=[VMEM] * len(operands),
        out_specs=[VMEM] * len(out_shape),
        out_shape=out_shape,
        compiler_params=params(16),
        cost_estimate=cost(1e6, 1 << 16),
        name="products_%d" % hop,
    )(*operands)


def finish_kernel(picks_ref, quality_ref, own_ref, norm_ref, g1, g2, g3, inverse_ref, out_ref, resid_ref, stage_ref, sent):
    total, width = own_ref.shape
    rounds, count = picks_ref.shape
    first_row = (lax.axis_index("rows") * (2 * X) + lax.axis_index("dim")) * width
    chosen = jnp.concatenate([as_column(picks_ref[r : r + 1, :]) for r in range(rounds)], axis=0) - first_row
    inverse = inverse_ref[...]
    tile = width // 3
    copies = []
    for i in range(3):
        here = pl.ds(i * tile, tile)
        values, norm = own_ref[:, here], norm_ref[:1, here]
        for ref in (g1, g2, g3):
            got = ref[:, here].astype(i32).astype(f32)
            scale = join(got[total + 2 : total + 3], got[total + 3 : total + 4] + 1.0)
            values = values + got[:total] * (scale * (1.0 / levels))
            norm = norm + join(got[total : total + 1], got[total + 1 : total + 2] + 0.5)
        lane = lax.broadcasted_iota(i32, (total, tile), 1) + i * tile
        values = jnp.where(chosen == lane, values + ridge_term, values)
        columns = jnp.dot(inverse, values, precision=HIGHEST, preferred_element_type=f32)
        score = quality_ref[here].reshape(1, tile)
        stage_ref[:, here] = columns * score
        copies.append(pltpu.make_async_copy(stage_ref.at[:, here], out_ref.at[:, here], sent.at[i]))
        copies[-1].start()
        left = norm + ridge_term - jnp.sum(columns * columns, axis=0, keepdims=True)
        resid_ref[here] = (score * score * left).reshape(tile)
    for copy in copies:
        copy.wait()


def finish(picks, quality, own, norm, got, inverse):
    total, width = own.shape
    return pl.pallas_call(
        finish_kernel,
        in_specs=[VMEM] * 8,
        out_specs=[ANY, VMEM],
        out_shape=[shape((total, width), f32), shape((width,), f32)],
        scratch_shapes=[pltpu.VMEM((total, width), f32), pltpu.SemaphoreType.DMA((3,))],
        compiler_params=params(16),
        cost_estimate=cost(12 * total * total * width, 4 << 20),
        name="finish",
    )(picks, quality, own, norm, *got, inverse)


def along_y(k):
    return [(r, r // Y * Y + (r % Y + k) % Y) for r in range(Y * Z)]


def along_z(partner):
    return [(r, partner(r // Y) * Y + r % Y) for r in range(Y * Z)]


def along_x(k):
    return [(d, (d // 2 + k) % X * 2 + d % 2) for d in range(2 * X)]


swap = [(d, d ^ 1) for d in range(2 * X)]
both_ways = [(d, (d // 2 + (1 if d % 2 == 0 else -1)) % X * 2 + d % 2) for d in range(2 * X)]


def per_device(embeddings, quality, picked_rows):
    total = picked_rows.size
    with jax.named_scope("swap_rows"):
        received = lax.ppermute(embeddings, "dim", swap)

    with jax.named_scope("gather_picks"):
        parts = local_picks(picked_rows, embeddings)
        mine = parts[0]
        for k in range(1, Y):
            mine = mine + lax.ppermute(parts[k], "rows", along_y(k))
        staged = {}
        mine = mine + lax.ppermute(mine, "rows", along_z(lambda z: z ^ 1))
        arrived = lax.ppermute(mine, "rows", along_z(lambda z: z ^ 2))
        *staged[2], mine = stage(2, embeddings, received, mine)
        mine = mine + arrived
        arrived = lax.ppermute(mine, "rows", along_z(lambda z: Z - 1 - z))
        *staged[1], mine = stage(1, embeddings, received, mine)
        mine = mine + arrived
        groups = [mine] + [lax.ppermute(mine, "rows", along_y(k)) for k in range(1, Y)]
        *staged[3], mine = stage(3, embeddings, received, mine)
        *staged[0], mine = stage(0, embeddings, received, mine)
        groups[0] = mine
        pick_mine = in_order(groups)
        pick_other = lax.ppermute(pick_mine, "dim", swap)

    full, half, keep = picks_gram(pick_mine, pick_other)
    got = {}
    with jax.named_scope("sum_gram"):
        near = lax.ppermute(full, "dim", both_ways)
        far = lax.ppermute(half, "dim", along_x(2))
        for hop in (2, 1):
            coded, keep = products(hop, staged[hop], pick_mine, pick_other, keep)
            got[hop] = lax.ppermute(coded, "dim", along_x(hop))
        gram = jnp.concatenate([keep[:128] + near[:128] + far, keep[128:] + near[128:]], axis=0)
        gram_other = lax.ppermute(gram, "dim", swap)
        coded, gram = products(3, staged[3], pick_mine, pick_other, gram)
        got[3] = lax.ppermute(coded, "dim", along_x(3))
    inverse = factor_inverse(gram, gram_other, total)
    own = products(0, staged[0], pick_mine, pick_other)[0]
    columns, residual = finish(picked_rows, quality, own, staged[0][2], [got[k] for k in (2, 1, 3)], inverse)
    return columns.T, residual


def solution(mesh):
    return jax.shard_map(
        per_device,
        mesh=mesh,
        in_specs=(P("rows", "dim"), P(("rows", "dim")), P()),
        out_specs=(P(("rows", "dim"), None), P(("rows", "dim"))),
        check_vma=False,
    )
```

```python
import functools

import jax
import jax.numpy as jnp
from jax import lax
from jax.experimental import pallas as pl
from jax.experimental.pallas import tpu as pltpu
from jax.sharding import PartitionSpec as P

ridge_term = 0.5
pack = 1152
Y, Z, X = 4, 8, 4
HIGHEST = lax.Precision.HIGHEST
NT = (((1,), (1,)), ((), ()))
TN = (((0,), (0,)), ((), ()))
f32, bf16, i32, i16 = jnp.float32, jnp.bfloat16, jnp.int32, jnp.int16
VMEM = pl.BlockSpec(memory_space=pltpu.VMEM)
ANY = pl.BlockSpec(memory_space=pl.ANY)
levels = 32767.0


def params(mib):
    return pltpu.CompilerParams(vmem_limit_bytes=mib << 20)


def cost(flops, nbytes):
    return pl.CostEstimate(flops=int(flops), bytes_accessed=int(nbytes), transcendentals=0)


def shape(dims, dtype):
    return jax.ShapeDtypeStruct(dims, dtype)


def as_column(row):
    n = row.shape[1]
    eye = lax.broadcasted_iota(i32, (n, n), 0) == lax.broadcasted_iota(i32, (n, n), 1)
    wide = jnp.broadcast_to(row.astype(f32), (n, n))
    return jnp.sum(jnp.where(eye, wide, 0.0), axis=1, keepdims=True).astype(i32)


def pick_kernel(picks_ref, e_ref, *rest):
    outs, (list_ref, tiles_ref, rows_ref, arrived) = rest[:Y], rest[Y:]
    rounds, count = picks_ref.shape
    total = rounds * count
    height = tiles_ref.shape[1]
    rows_here = e_ref.shape[0]
    row_start = lax.axis_index("rows") * rows_here
    held = jnp.int32(0)
    for p in range(total):
        local = picks_ref[p // count, p % count] - row_start
        list_ref[held] = local * 256 + p
        held = held + jnp.where((local >= 0) & (local < rows_here), 1, 0)

    def fetch(i):
        tile = pl.multiple_of(lax.div(list_ref[i], 256 * height) * height, height)
        return pltpu.make_async_copy(e_ref.at[pl.ds(tile, height), :], tiles_ref.at[i], arrived.at[i])

    def begin(i, carry):
        fetch(i).start()
        return carry

    def end(i, carry):
        fetch(i).wait()
        sub = lax.broadcasted_iota(i32, tiles_ref.shape[1:], 0)
        place, p = lax.div(list_ref[i], 256), lax.rem(list_ref[i], 256)
        one = jnp.where(sub == lax.rem(place, height), tiles_ref[i].astype(f32), 0.0)
        rows_ref[pl.ds(p, 1), :] = jnp.sum(one, axis=0, keepdims=True)
        return carry

    lax.fori_loop(0, held, begin, 0)
    rows_ref[...] = jnp.zeros_like(rows_ref)
    lax.fori_loop(0, held, end, 0)
    y = lax.rem(lax.axis_index("rows"), Y)
    group = total // Y
    for j in range(Y):
        g = lax.bitwise_xor(y, j)
        outs[j][...] = rows_ref[pl.ds(pl.multiple_of(g * group, 16), group), :].astype(bf16)


def local_picks(picks, embeddings):
    dims = embeddings.shape[1]
    total = picks.size
    return pl.pallas_call(
        pick_kernel,
        in_specs=[pl.BlockSpec(memory_space=pltpu.SMEM), ANY],
        out_specs=[VMEM] * Y,
        out_shape=[shape((total // Y, dims), bf16)] * Y,
        scratch_shapes=[
            pltpu.SMEM((256,), i32),
            pltpu.VMEM((total, 16, dims), bf16),
            pltpu.VMEM((total, dims), f32),
            pltpu.SemaphoreType.DMA((total,)),
        ],
        compiler_params=params(50),
        cost_estimate=cost(0, 10 << 20),
        name="local_picks",
    )(picks, embeddings)


def fetch_rows(hop, e_ref, r_ref, mine_ref, other_ref, arrived):
    d = lax.axis_index("dim")
    chip, core = lax.div(d, 2), lax.rem(d, 2)
    first = (lax.rem(chip + hop, X) * 2 + core) * pack
    tile = pack // 3
    copies = []
    for i in range(3):
        there, here = pl.ds(pl.multiple_of(first + i * tile, 128), tile), pl.ds(i * tile, tile)
        copies.append(
            (
                pltpu.make_async_copy(e_ref.at[there, :], mine_ref.at[here, :], arrived.at[2 * i]),
                pltpu.make_async_copy(r_ref.at[there, :], other_ref.at[here, :], arrived.at[2 * i + 1]),
            )
        )
    for pair in copies:
        for copy in pair:
            copy.start()
    return copies


def squared_norms(i, mine_ref, other_ref):
    tile = pack // 3
    squares = jnp.zeros((tile, 128), f32)
    for ref in (mine_ref, other_ref):
        for j in range(0, ref.shape[1], 128):
            part = ref[i * tile : (i + 1) * tile, j : j + 128].astype(f32)
            squares += part * part
    high = squares.astype(bf16)
    low = (squares - high.astype(f32)).astype(bf16)
    ones = jnp.ones((8, 128), bf16)
    norm = lax.dot_general(ones, high, NT, preferred_element_type=f32)
    return norm + lax.dot_general(ones, low, NT, preferred_element_type=f32)


def stage_kernel(hop, e_ref, r_ref, through_ref, mine_ref, other_ref, norm_ref, passed_ref, arrived):
    copies = fetch_rows(hop, e_ref, r_ref, mine_ref, other_ref, arrived)
    passed_ref[...] = through_ref[...]
    tile = pack // 3
    for i in range(3):
        for copy in copies[i]:
            copy.wait()
        norm_ref[:, i * tile : (i + 1) * tile] = squared_norms(i, mine_ref, other_ref)


def stage(hop, embeddings, received, through):
    dims = embeddings.shape[1]
    return pl.pallas_call(
        functools.partial(stage_kernel, hop),
        in_specs=[ANY, ANY, VMEM],
        out_specs=[VMEM] * 4,
        out_shape=[
            shape((pack, dims), bf16),
            shape((pack, dims), bf16),
            shape((8, pack), f32),
            shape(through.shape, through.dtype),
        ],
        scratch_shapes=[pltpu.SemaphoreType.DMA((6,))],
        compiler_params=params(50),
        cost_estimate=cost(0, 4 * pack * dims),
        name="stage_%d" % hop,
    )(embeddings, received, through)


def order_kernel(s0, s1, s2, s3, out_ref):
    y = lax.rem(lax.axis_index("rows"), Y)
    group = s0.shape[0]
    for j, ref in enumerate((s0, s1, s2, s3)):
        g = pl.multiple_of(lax.bitwise_xor(y, j) * group, 16)
        out_ref[pl.ds(g, group), :] = ref[...]


def in_order(groups):
    group, dims = groups[0].shape
    return pl.pallas_call(
        order_kernel,
        in_specs=[VMEM] * Y,
        out_specs=VMEM,
        out_shape=shape((group * Y, dims), bf16),
        compiler_params=params(16),
        cost_estimate=cost(0, 4 * Y * group * dims),
        name="order",
    )(*groups)


def gram_kernel(mine_ref, other_ref, token_ref, full_ref, half_ref, keep_ref):
    mine, other = mine_ref[...], other_ref[...]
    gram = lax.dot_general(mine, mine, NT, preferred_element_type=f32)
    gram += lax.dot_general(other, other, NT, preferred_element_type=f32)
    core = lax.rem(lax.axis_index("dim"), 2)
    top = gram[:128, :128]
    corner = jnp.concatenate([gram[128:, 128:], jnp.zeros((64, 64), f32)], axis=1)
    low = jnp.concatenate([gram[128:, :128], corner], axis=0)
    a, b = jnp.where(core == 0, top, low), jnp.where(core == 0, low, top)
    half_ref[...] = a
    full_ref[:128, :], full_ref[128:, :] = a, b
    keep_ref[:128, :], keep_ref[128:, :] = jnp.where(core == 0, a, 0.0), jnp.where(core == 0, b, 0.0)


def picks_gram(mine, other, token):
    total, dims = mine.shape
    return pl.pallas_call(
        gram_kernel,
        in_specs=[VMEM] * 3,
        out_specs=[VMEM] * 3,
        out_shape=[shape((256, 128), f32), shape((128, 128), f32), shape((256, 128), f32)],
        compiler_params=params(16),
        cost_estimate=cost(4 * total * total * dims, 4 * total * dims),
        name="gram",
    )(mine, other, token)


panel, together = 64, 8


def factor_kernel(sum_ref, swapped_ref, high_ref, low_ref, m_ref):
    n = high_ref.shape[0]
    core = lax.rem(lax.axis_index("dim"), 2)
    a = sum_ref[:128, :] + swapped_ref[128:, :]
    b = sum_ref[128:, :] + swapped_ref[:128, :]
    first, last = jnp.where(core == 0, a, b), jnp.where(core == 0, b, a)
    width = m_ref.shape[1]
    sub = lax.broadcasted_iota(i32, (n, width - 128), 0)
    lane = lax.broadcasted_iota(i32, (n, width - 128), 1) + 128
    m_ref[:, 128:] = jnp.where(lane - n == sub, 1.0, 0.0)
    diag = lax.broadcasted_iota(i32, (128, 128), 0) == lax.broadcasted_iota(i32, (128, 128), 1)
    ridge = jnp.where(diag, ridge_term, 0.0)
    m_ref[:128, :128] = first + ridge
    m_ref[128:, :128] = last[:64, :]
    m_ref[128:, 128:n] = last[64:, :64] + ridge[:64, :64]
    m_ref[:128, 128:n] = last[:64, :].T
    below = lax.broadcasted_iota(i32, (panel, 128), 0)
    at = lax.broadcasted_iota(i32, (panel, 128), 1) - below
    for low in range(0, n, panel):
        left = low // 128 * 128
        off = low - left
        tiles = [m_ref[low : low + panel, j : j + 128] for j in range(left, width, 128)]
        for g in range(0, panel, together):
            cols = [
                jnp.broadcast_to(tiles[0][:, off + g + i : off + g + i + 1], (panel, 128)) for i in range(together)
            ]
            heads = [[t[g + i : g + i + 1, :] for t in tiles] for i in range(together)]
            for i in range(together):
                factors = jnp.where(below > g + i, cols[i] * (1.0 / cols[i][g + i : g + i + 1, :]), 0.0)
                for j in range(i + 1, together):
                    cols[j] = cols[j] - factors * cols[j][g + i : g + i + 1, :]
                    by = factors[g + j : g + j + 1, :]
                    heads[j] = [x - by * y for x, y in zip(heads[j], heads[i])]
                tiles = [t - factors * y for t, y in zip(tiles, heads[i])]
        pivots = jnp.sum(jnp.where(at == off, tiles[0], 0.0), axis=1, keepdims=True)
        rows = jnp.concatenate(tiles, axis=1) * (1.0 / jnp.sqrt(pivots))
        inverse = rows[:, n - left :]
        high = inverse.astype(bf16)
        high_ref[low : low + panel, :] = high
        low_ref[low : low + panel, :] = (inverse - high.astype(f32)).astype(bf16)
        if low + panel < n:
            update = lax.dot_general(rows[:, : n - left], rows, TN, precision=HIGHEST, preferred_element_type=f32)
            m_ref[low + panel :, left:] -= update[low + panel - left :, :]


def factor_inverse(total, swapped, n):
    return pl.pallas_call(
        factor_kernel,
        in_specs=[VMEM] * 2,
        out_specs=[VMEM] * 2,
        out_shape=[shape((n, n), bf16)] * 2,
        scratch_shapes=[pltpu.VMEM((n, 2 * n), f32)],
        compiler_params=params(16),
        cost_estimate=cost(1e6, 1 << 16),
        name="factor",
    )(total, swapped)


def split(value):
    scaled = value * 16.0
    high = jnp.floor(scaled)
    return high, jnp.floor((scaled - high) * 32768.0)


def join(high, low):
    return (high + low * (1.0 / 32768.0)) * (1.0 / 16.0)


def block_products(at, e_ref, r_ref, mine_ref, other_ref):
    part = lax.dot_general(mine_ref[...], e_ref[at, :], NT, preferred_element_type=f32)
    return part + lax.dot_general(other_ref[...], r_ref[at, :], NT, preferred_element_type=f32)


def coded(part, norm):
    norm_high, norm_low = split(norm)
    top_high, top_low = split(jnp.max(jnp.abs(part), axis=0, keepdims=True))
    scale = join(top_high, top_low + 1.0)
    whole = jnp.floor(part * (levels / scale) + 0.5)
    row = lax.broadcasted_iota(i32, (8, part.shape[1]), 0)
    extra = jnp.where(row == 0, norm_high, jnp.where(row == 1, norm_low, jnp.where(row == 2, top_high, top_low)))
    return jnp.concatenate([whole, extra], axis=0).astype(i32).astype(i16)


def decoded(ref, at, total):
    got = ref[:, at].astype(i32).astype(f32)
    scale = join(got[total + 2 : total + 3], got[total + 3 : total + 4] + 1.0)
    norm = join(got[total : total + 1], got[total + 1 : total + 2] + 0.5)
    return got[:total] * (scale * (1.0 / levels)), norm


cut = 640
spans = ((0, 384), (384, 256), (640, 512))


def far_kernel(e_ref, r_ref, norm_ref, mine_ref, other_ref, low_ref, high_ref, token_ref):
    for low, width in spans:
        at = pl.ds(low, width)
        part = block_products(at, e_ref, r_ref, mine_ref, other_ref)
        out = coded(part, norm_ref[:1, at])
        if low < cut:
            low_ref[:, at] = out
        else:
            high_ref[:, low - cut : low - cut + width] = out
    token_ref[...] = jnp.zeros_like(token_ref)


def both_kernel(e_next, r_next, e_last, r_last, mine_ref, other_ref, through_ref, next_ref, last_ref, passed_ref):
    passed_ref[...] = through_ref[...]
    for low, width in spans:
        at = pl.ds(low, width)
        next_ref[:, at] = block_products(at, e_next, r_next, mine_ref, other_ref)
        last_ref[:, at] = block_products(at, e_last, r_last, mine_ref, other_ref)


def near_kernel(begin, end, part_ref, norm_ref, got_ref, through_ref, out_ref, passed_ref):
    total = part_ref.shape[0]
    passed_ref[...] = through_ref[...]
    for low, width in spans:
        at = pl.ds(low, width)
        part, norm = part_ref[:, at], norm_ref[:1, at]
        if begin <= low < end:
            more, more_norm = decoded(got_ref, pl.ds(low - begin, width), total)
            part, norm = part + more, norm + more_norm
        out_ref[:, at] = coded(part, norm)


def own_kernel(
    picks_ref, e_ref, r_ref, mine_ref, other_ref, through_ref, out_ref, norm_ref, passed_ref, e_here, r_here, arrived
):
    copies = fetch_rows(0, e_ref, r_ref, e_here, r_here, arrived)
    passed_ref[...] = through_ref[...]
    rounds, count = picks_ref.shape
    first_row = (lax.axis_index("rows") * (2 * X) + lax.axis_index("dim")) * pack
    chosen = jnp.concatenate([as_column(picks_ref[r : r + 1, :]) for r in range(rounds)], axis=0) - first_row
    tile = pack // 3
    for i in range(3):
        for copy in copies[i]:
            copy.wait()
        at = slice(i * tile, (i + 1) * tile)
        norm_ref[:, at] = squared_norms(i, e_here, r_here)
        part = block_products(pl.ds(i * tile, tile), e_here, r_here, mine_ref, other_ref)
        lane = lax.broadcasted_iota(i32, part.shape, 1) + i * tile
        out_ref[:, at] = jnp.where(chosen == lane, part + ridge_term, part)


def quick(kernel, name, in_specs, out_shape, mib=16, scratch=(), flops=1e6):
    return pl.pallas_call(
        kernel,
        in_specs=in_specs,
        out_specs=[VMEM] * len(out_shape),
        out_shape=out_shape,
        scratch_shapes=scratch,
        compiler_params=params(mib),
        cost_estimate=cost(flops, 1 << 16),
        name=name,
    )


def far_products(staged, mine, other):
    total = mine.shape[0]
    out_shape = [shape((total + 8, cut), i16), shape((total + 8, pack - cut), i16), shape((8, 128), f32)]
    return quick(far_kernel, "products_far", [VMEM] * 5, out_shape)(*staged, mine, other)


def both_products(following, last, mine, other, through):
    total = mine.shape[0]
    out_shape = [shape((total, pack), f32)] * 2 + [shape(through.shape, through.dtype)]
    return quick(both_kernel, "products_both", [VMEM] * 7, out_shape)(*following[:2], *last[:2], mine, other, through)


def near_block(begin, end, part, norm, got, through):
    out_shape = [shape((part.shape[0] + 8, pack), i16), shape(through.shape, through.dtype)]
    kernel = functools.partial(near_kernel, begin, end)
    return quick(kernel, "near_%d" % begin, [VMEM] * 4, out_shape)(part, norm, got, through)


def own_products(picks, embeddings, received, mine, other, through):
    total, dims = mine.shape
    out_shape = [shape((total, pack), f32), shape((8, pack), f32), shape(through.shape, through.dtype)]
    scratch = [pltpu.VMEM((pack, dims), bf16), pltpu.VMEM((pack, dims), bf16), pltpu.SemaphoreType.DMA((6,))]
    in_specs = [VMEM, ANY, ANY, VMEM, VMEM, VMEM]
    call = quick(own_kernel, "products_own", in_specs, out_shape, 46, scratch)
    return call(picks, embeddings, received, mine, other, through)


def finish_kernel(quality_ref, own_ref, norm_ref, g1, g2, inv_high, inv_low, out_ref, resid_ref, stage_ref, sent):
    total, width = own_ref.shape
    inverse_high, inverse_low = inv_high[...], inv_low[...]
    tile = width // 3
    copies = []
    for i in range(3):
        here = pl.ds(i * tile, tile)
        values, norm = own_ref[:, here], norm_ref[:1, here]
        for ref in (g1, g2):
            more, more_norm = decoded(ref, here, total)
            values, norm = values + more, norm + more_norm
        high = values.astype(bf16)
        low = (values - high.astype(f32)).astype(bf16)
        columns = jnp.dot(inverse_high, high, preferred_element_type=f32)
        columns += jnp.dot(inverse_high, low, preferred_element_type=f32)
        columns += jnp.dot(inverse_low, high, preferred_element_type=f32)
        score = quality_ref[here].reshape(1, tile)
        stage_ref[:, here] = columns * score
        copies.append(pltpu.make_async_copy(stage_ref.at[:, here], out_ref.at[:, here], sent.at[i]))
        copies[-1].start()
        left = norm + ridge_term - jnp.sum(columns * columns, axis=0, keepdims=True)
        resid_ref[here] = (score * score * left).reshape(tile)
    for copy in copies:
        copy.wait()


def finish(quality, own, norm, got, inverse):
    total, width = own.shape
    return pl.pallas_call(
        finish_kernel,
        in_specs=[VMEM] * 7,
        out_specs=[ANY, VMEM],
        out_shape=[shape((total, width), f32), shape((width,), f32)],
        scratch_shapes=[pltpu.VMEM((total, width), f32), pltpu.SemaphoreType.DMA((3,))],
        compiler_params=params(16),
        cost_estimate=cost(12 * total * total * width, 4 << 20),
        name="finish",
    )(quality, own, norm, *got, *inverse)


def along_y(k):
    return [(r, r ^ k) for r in range(Y * Z)]


def along_z(partner):
    return [(r, partner(r // Y) * Y + r % Y) for r in range(Y * Z)]


def along_x(k):
    return [(d, (d // 2 + k) % X * 2 + d % 2) for d in range(2 * X)]


swap = [(d, d ^ 1) for d in range(2 * X)]
both_ways = [(d, (d // 2 + (1 if d % 2 == 0 else -1)) % X * 2 + d % 2) for d in range(2 * X)]


def per_device(embeddings, quality, picked_rows):
    total = picked_rows.size
    with jax.named_scope("swap_rows"):
        received = lax.ppermute(embeddings, "dim", swap)

    with jax.named_scope("gather_picks"):
        parts = local_picks(picked_rows, embeddings)
        mine = parts[0]
        for k in range(1, Y):
            mine = mine + lax.ppermute(parts[k], "rows", along_y(k))
        staged = {}
        mine = mine + lax.ppermute(mine, "rows", along_z(lambda z: z ^ 1))
        arrived = lax.ppermute(mine, "rows", along_z(lambda z: z ^ 2))
        *staged[2], mine = stage(2, embeddings, received, mine)
        mine = mine + arrived
        arrived = lax.ppermute(mine, "rows", along_z(lambda z: z ^ 6))
        *staged[1], mine = stage(1, embeddings, received, mine)
        mine = mine + arrived
        groups = [mine] + [lax.ppermute(mine, "rows", along_y(k)) for k in range(1, Y)]
        *staged[3], mine = stage(3, embeddings, received, mine)
        groups[0] = mine
        pick_mine = in_order(groups)
        pick_other = lax.ppermute(pick_mine, "dim", swap)

    with jax.named_scope("sum_products"):
        to_next, to_last, token = far_products(staged[2], pick_mine, pick_other)
        from_last = lax.ppermute(to_next, "dim", along_x(1))
        from_next = lax.ppermute(to_last, "dim", along_x(3))
        full, half, keep = picks_gram(pick_mine, pick_other, token)
        gram_near = lax.ppermute(full, "dim", both_ways)
        gram_far = lax.ppermute(half, "dim", along_x(2))
        for_next, for_last, keep = both_products(staged[1], staged[3], pick_mine, pick_other, keep)
        onward, keep = near_block(0, cut, for_next, staged[1][2], from_last, keep)
        got_last = lax.ppermute(onward, "dim", along_x(1))
        onward, keep = near_block(cut, pack, for_last, staged[3][2], from_next, keep)
        got_next = lax.ppermute(onward, "dim", along_x(3))
    with jax.named_scope("sum_gram"):
        gram = jnp.concatenate([keep[:128] + gram_near[:128] + gram_far, keep[128:] + gram_near[128:]], axis=0)
        gram_other = lax.ppermute(gram, "dim", swap)
    own, norm, gram = own_products(picked_rows, embeddings, received, pick_mine, pick_other, gram)
    inverse = factor_inverse(gram, gram_other, total)
    columns, residual = finish(quality, own, norm, [got_last, got_next], inverse)
    return columns.T, residual


def solution(mesh):
    return jax.shard_map(
        per_device,
        mesh=mesh,
        in_specs=(P("rows", "dim"), P(("rows", "dim")), P()),
        out_specs=(P(("rows", "dim"), None), P(("rows", "dim"))),
        check_vma=False,
    )
```

```python
import functools

import jax
import jax.numpy as jnp
from jax import lax
from jax.experimental import pallas as pl
from jax.experimental.pallas import tpu as pltpu
from jax.sharding import PartitionSpec as P

ridge_term = 0.5
pack = 1152
Y, Z, X = 4, 8, 4
HIGHEST = lax.Precision.HIGHEST
NT = (((1,), (1,)), ((), ()))
TN = (((0,), (0,)), ((), ()))
f32, bf16, i32, i16 = jnp.float32, jnp.bfloat16, jnp.int32, jnp.int16
VMEM = pl.BlockSpec(memory_space=pltpu.VMEM)
ANY = pl.BlockSpec(memory_space=pl.ANY)
levels = 32767.0


def params(mib):
    return pltpu.CompilerParams(vmem_limit_bytes=mib << 20)


def cost(flops, nbytes):
    return pl.CostEstimate(flops=int(flops), bytes_accessed=int(nbytes), transcendentals=0)


def shape(dims, dtype):
    return jax.ShapeDtypeStruct(dims, dtype)


def as_column(row):
    n = row.shape[1]
    eye = lax.broadcasted_iota(i32, (n, n), 0) == lax.broadcasted_iota(i32, (n, n), 1)
    wide = jnp.broadcast_to(row.astype(f32), (n, n))
    return jnp.sum(jnp.where(eye, wide, 0.0), axis=1, keepdims=True).astype(i32)


def pick_kernel(picks_ref, e_ref, *rest):
    outs, (list_ref, tiles_ref, rows_ref, arrived) = rest[:Y], rest[Y:]
    rounds, count = picks_ref.shape
    total = rounds * count
    height = tiles_ref.shape[1]
    rows_here = e_ref.shape[0]
    row_start = lax.axis_index("rows") * rows_here
    held = jnp.int32(0)
    for p in range(total):
        local = picks_ref[p // count, p % count] - row_start
        list_ref[held] = local * 256 + p
        held = held + jnp.where((local >= 0) & (local < rows_here), 1, 0)

    def fetch(i):
        tile = pl.multiple_of(lax.div(list_ref[i], 256 * height) * height, height)
        return pltpu.make_async_copy(e_ref.at[pl.ds(tile, height), :], tiles_ref.at[i], arrived.at[i])

    def begin(i, carry):
        fetch(i).start()
        return carry

    def end(i, carry):
        fetch(i).wait()
        sub = lax.broadcasted_iota(i32, tiles_ref.shape[1:], 0)
        place, p = lax.div(list_ref[i], 256), lax.rem(list_ref[i], 256)
        one = jnp.where(sub == lax.rem(place, height), tiles_ref[i].astype(f32), 0.0)
        rows_ref[pl.ds(p, 1), :] = jnp.sum(one, axis=0, keepdims=True)
        return carry

    lax.fori_loop(0, held, begin, 0)
    rows_ref[...] = jnp.zeros_like(rows_ref)
    lax.fori_loop(0, held, end, 0)
    y = lax.rem(lax.axis_index("rows"), Y)
    group = total // Y
    for j in range(Y):
        g = lax.bitwise_xor(y, j)
        outs[j][...] = rows_ref[pl.ds(pl.multiple_of(g * group, 16), group), :].astype(bf16)


def local_picks(picks, embeddings):
    dims = embeddings.shape[1]
    total = picks.size
    return pl.pallas_call(
        pick_kernel,
        in_specs=[pl.BlockSpec(memory_space=pltpu.SMEM), ANY],
        out_specs=[VMEM] * Y,
        out_shape=[shape((total // Y, dims), bf16)] * Y,
        scratch_shapes=[
            pltpu.SMEM((256,), i32),
            pltpu.VMEM((total, 16, dims), bf16),
            pltpu.VMEM((total, dims), f32),
            pltpu.SemaphoreType.DMA((total,)),
        ],
        compiler_params=params(50),
        cost_estimate=cost(0, 10 << 20),
        name="local_picks",
    )(picks, embeddings)


def fetch_rows(hop, e_ref, r_ref, mine_ref, other_ref, arrived):
    d = lax.axis_index("dim")
    chip, core = lax.div(d, 2), lax.rem(d, 2)
    first = (lax.rem(chip + hop, X) * 2 + core) * pack
    tile = pack // 3
    copies = []
    for i in range(3):
        there, here = pl.ds(pl.multiple_of(first + i * tile, 128), tile), pl.ds(i * tile, tile)
        copies.append(
            (
                pltpu.make_async_copy(e_ref.at[there, :], mine_ref.at[here, :], arrived.at[2 * i]),
                pltpu.make_async_copy(r_ref.at[there, :], other_ref.at[here, :], arrived.at[2 * i + 1]),
            )
        )
    for pair in copies:
        for copy in pair:
            copy.start()
    return copies


def squared_norms(i, mine_ref, other_ref):
    tile = pack // 3
    squares = jnp.zeros((tile, 128), f32)
    for ref in (mine_ref, other_ref):
        for j in range(0, ref.shape[1], 128):
            part = ref[i * tile : (i + 1) * tile, j : j + 128].astype(f32)
            squares += part * part
    high = squares.astype(bf16)
    low = (squares - high.astype(f32)).astype(bf16)
    ones = jnp.ones((8, 128), bf16)
    norm = lax.dot_general(ones, high, NT, preferred_element_type=f32)
    return norm + lax.dot_general(ones, low, NT, preferred_element_type=f32)


def stage_kernel(hop, e_ref, r_ref, through_ref, mine_ref, other_ref, norm_ref, passed_ref, arrived):
    copies = fetch_rows(hop, e_ref, r_ref, mine_ref, other_ref, arrived)
    passed_ref[...] = through_ref[...]
    tile = pack // 3
    for i in range(3):
        for copy in copies[i]:
            copy.wait()
        norm_ref[:, i * tile : (i + 1) * tile] = squared_norms(i, mine_ref, other_ref)


def stage(hop, embeddings, received, through):
    dims = embeddings.shape[1]
    return pl.pallas_call(
        functools.partial(stage_kernel, hop),
        in_specs=[ANY, ANY, VMEM],
        out_specs=[VMEM] * 4,
        out_shape=[
            shape((pack, dims), bf16),
            shape((pack, dims), bf16),
            shape((8, pack), f32),
            shape(through.shape, through.dtype),
        ],
        scratch_shapes=[pltpu.SemaphoreType.DMA((6,))],
        compiler_params=params(50),
        cost_estimate=cost(0, 4 * pack * dims),
        name="stage_%d" % hop,
    )(embeddings, received, through)


def order_kernel(s0, s1, s2, s3, out_ref):
    y = lax.rem(lax.axis_index("rows"), Y)
    group = s0.shape[0]
    for j, ref in enumerate((s0, s1, s2, s3)):
        g = pl.multiple_of(lax.bitwise_xor(y, j) * group, 16)
        out_ref[pl.ds(g, group), :] = ref[...]


def in_order(groups):
    group, dims = groups[0].shape
    return pl.pallas_call(
        order_kernel,
        in_specs=[VMEM] * Y,
        out_specs=VMEM,
        out_shape=shape((group * Y, dims), bf16),
        compiler_params=params(16),
        cost_estimate=cost(0, 4 * Y * group * dims),
        name="order",
    )(*groups)


def gram_kernel(mine_ref, other_ref, token_ref, full_ref, half_ref, keep_ref):
    mine, other = mine_ref[...], other_ref[...]
    gram = lax.dot_general(mine, mine, NT, preferred_element_type=f32)
    gram += lax.dot_general(other, other, NT, preferred_element_type=f32)
    core = lax.rem(lax.axis_index("dim"), 2)
    top = gram[:128, :128]
    corner = jnp.concatenate([gram[128:, 128:], jnp.zeros((64, 64), f32)], axis=1)
    low = jnp.concatenate([gram[128:, :128], corner], axis=0)
    a, b = jnp.where(core == 0, top, low), jnp.where(core == 0, low, top)
    half_ref[...] = a
    full_ref[:128, :], full_ref[128:, :] = a, b
    keep_ref[:128, :], keep_ref[128:, :] = jnp.where(core == 0, a, 0.0), jnp.where(core == 0, b, 0.0)


def picks_gram(mine, other, token):
    total, dims = mine.shape
    return pl.pallas_call(
        gram_kernel,
        in_specs=[VMEM] * 3,
        out_specs=[VMEM] * 3,
        out_shape=[shape((256, 128), f32), shape((128, 128), f32), shape((256, 128), f32)],
        compiler_params=params(16),
        cost_estimate=cost(4 * total * total * dims, 4 * total * dims),
        name="gram",
    )(mine, other, token)


panel, together = 64, 8


def factor_kernel(sum_ref, swapped_ref, high_ref, low_ref, m_ref):
    n = high_ref.shape[0]
    core = lax.rem(lax.axis_index("dim"), 2)
    a = sum_ref[:128, :] + swapped_ref[128:, :]
    b = sum_ref[128:, :] + swapped_ref[:128, :]
    first, last = jnp.where(core == 0, a, b), jnp.where(core == 0, b, a)
    width = m_ref.shape[1]
    sub = lax.broadcasted_iota(i32, (n, width - 128), 0)
    lane = lax.broadcasted_iota(i32, (n, width - 128), 1) + 128
    m_ref[:, 128:] = jnp.where(lane - n == sub, 1.0, 0.0)
    diag = lax.broadcasted_iota(i32, (128, 128), 0) == lax.broadcasted_iota(i32, (128, 128), 1)
    ridge = jnp.where(diag, ridge_term, 0.0)
    m_ref[:128, :128] = first + ridge
    m_ref[128:, :128] = last[:64, :]
    m_ref[128:, 128:n] = last[64:, :64] + ridge[:64, :64]
    m_ref[:128, 128:n] = last[:64, :].T
    below = lax.broadcasted_iota(i32, (panel, 128), 0)
    at = lax.broadcasted_iota(i32, (panel, 128), 1) - below
    for low in range(0, n, panel):
        left = low // 128 * 128
        off = low - left
        tiles = [m_ref[low : low + panel, j : j + 128] for j in range(left, width, 128)]
        for g in range(0, panel, together):
            cols = [
                jnp.broadcast_to(tiles[0][:, off + g + i : off + g + i + 1], (panel, 128)) for i in range(together)
            ]
            heads = [[t[g + i : g + i + 1, :] for t in tiles] for i in range(together)]
            for i in range(together):
                factors = jnp.where(below > g + i, cols[i] * (1.0 / cols[i][g + i : g + i + 1, :]), 0.0)
                for j in range(i + 1, together):
                    cols[j] = cols[j] - factors * cols[j][g + i : g + i + 1, :]
                    by = factors[g + j : g + j + 1, :]
                    heads[j] = [x - by * y for x, y in zip(heads[j], heads[i])]
                tiles = [t - factors * y for t, y in zip(tiles, heads[i])]
        pivots = jnp.sum(jnp.where(at == off, tiles[0], 0.0), axis=1, keepdims=True)
        rows = jnp.concatenate(tiles, axis=1) * (1.0 / jnp.sqrt(pivots))
        inverse = rows[:, n - left :]
        high = inverse.astype(bf16)
        high_ref[low : low + panel, :] = high
        low_ref[low : low + panel, :] = (inverse - high.astype(f32)).astype(bf16)
        if low + panel < n:
            update = lax.dot_general(rows[:, : n - left], rows, TN, precision=HIGHEST, preferred_element_type=f32)
            m_ref[low + panel :, left:] -= update[low + panel - left :, :]


def factor_inverse(total, swapped, n):
    return pl.pallas_call(
        factor_kernel,
        in_specs=[VMEM] * 2,
        out_specs=[VMEM] * 2,
        out_shape=[shape((n, n), bf16)] * 2,
        scratch_shapes=[pltpu.VMEM((n, 2 * n), f32)],
        compiler_params=params(16),
        cost_estimate=cost(1e6, 1 << 16),
        name="factor",
    )(total, swapped)


def split(value):
    scaled = value * 16.0
    high = jnp.floor(scaled)
    return high, jnp.floor((scaled - high) * 32768.0)


def join(high, low):
    return (high + low * (1.0 / 32768.0)) * (1.0 / 16.0)


def block_products(at, e_ref, r_ref, mine_ref, other_ref):
    part = lax.dot_general(mine_ref[...], e_ref[at, :], NT, preferred_element_type=f32)
    return part + lax.dot_general(other_ref[...], r_ref[at, :], NT, preferred_element_type=f32)


def coded(part, norm):
    norm_high, norm_low = split(norm)
    top_high, top_low = split(jnp.max(jnp.abs(part), axis=0, keepdims=True))
    scale = join(top_high, top_low + 1.0)
    whole = jnp.floor(part * (levels / scale) + 0.5)
    row = lax.broadcasted_iota(i32, (8, part.shape[1]), 0)
    extra = jnp.where(row == 0, norm_high, jnp.where(row == 1, norm_low, jnp.where(row == 2, top_high, top_low)))
    return jnp.concatenate([whole, extra], axis=0).astype(i32).astype(i16)


def decoded(ref, at, total):
    got = ref[:, at].astype(i32).astype(f32)
    scale = join(got[total + 2 : total + 3], got[total + 3 : total + 4] + 1.0)
    norm = join(got[total : total + 1], got[total + 1 : total + 2] + 0.5)
    return got[:total] * (scale * (1.0 / levels)), norm


cut = 640
spans = ((0, 384), (384, 256), (640, 512))


def far_kernel(e_ref, r_ref, norm_ref, mine_ref, other_ref, low_ref, high_ref, token_ref):
    for low, width in spans:
        at = pl.ds(low, width)
        part = block_products(at, e_ref, r_ref, mine_ref, other_ref)
        out = coded(part, norm_ref[:1, at])
        if low < cut:
            low_ref[:, at] = out
        else:
            high_ref[:, low - cut : low - cut + width] = out
    token_ref[...] = jnp.zeros_like(token_ref)


def both_kernel(e_next, r_next, e_last, r_last, mine_ref, other_ref, through_ref, next_ref, last_ref, passed_ref):
    passed_ref[...] = through_ref[...]
    for low, width in spans:
        at = pl.ds(low, width)
        next_ref[:, at] = block_products(at, e_next, r_next, mine_ref, other_ref)
        last_ref[:, at] = block_products(at, e_last, r_last, mine_ref, other_ref)


def near_kernel(begin, end, part_ref, norm_ref, got_ref, through_ref, out_ref, passed_ref):
    total = part_ref.shape[0]
    passed_ref[...] = through_ref[...]
    for low, width in spans:
        at = pl.ds(low, width)
        part, norm = part_ref[:, at], norm_ref[:1, at]
        if begin <= low < end:
            more, more_norm = decoded(got_ref, pl.ds(low - begin, width), total)
            part, norm = part + more, norm + more_norm
        out_ref[:, at] = coded(part, norm)


def own_kernel(
    picks_ref, e_ref, r_ref, mine_ref, other_ref, through_ref, out_ref, norm_ref, passed_ref, e_here, r_here, arrived
):
    copies = fetch_rows(0, e_ref, r_ref, e_here, r_here, arrived)
    passed_ref[...] = through_ref[...]
    rounds, count = picks_ref.shape
    first_row = (lax.axis_index("rows") * (2 * X) + lax.axis_index("dim")) * pack
    chosen = jnp.concatenate([as_column(picks_ref[r : r + 1, :]) for r in range(rounds)], axis=0) - first_row
    tile = pack // 3
    for i in range(3):
        for copy in copies[i]:
            copy.wait()
        at = slice(i * tile, (i + 1) * tile)
        norm_ref[:, at] = squared_norms(i, e_here, r_here)
        part = block_products(pl.ds(i * tile, tile), e_here, r_here, mine_ref, other_ref)
        lane = lax.broadcasted_iota(i32, part.shape, 1) + i * tile
        out_ref[:, at] = jnp.where(chosen == lane, part + ridge_term, part)


def quick(kernel, name, in_specs, out_shape, mib=16, scratch=(), flops=1e6):
    return pl.pallas_call(
        kernel,
        in_specs=in_specs,
        out_specs=[VMEM] * len(out_shape),
        out_shape=out_shape,
        scratch_shapes=scratch,
        compiler_params=params(mib),
        cost_estimate=cost(flops, 1 << 16),
        name=name,
    )


def far_products(staged, mine, other):
    total = mine.shape[0]
    out_shape = [shape((total + 8, cut), i16), shape((total + 8, pack - cut), i16), shape((8, 128), f32)]
    return quick(far_kernel, "products_far", [VMEM] * 5, out_shape)(*staged, mine, other)


def both_products(following, last, mine, other, through):
    total = mine.shape[0]
    out_shape = [shape((total, pack), f32)] * 2 + [shape(through.shape, through.dtype)]
    return quick(both_kernel, "products_both", [VMEM] * 7, out_shape)(*following[:2], *last[:2], mine, other, through)


def near_block(begin, end, part, norm, got, through):
    out_shape = [shape((part.shape[0] + 8, pack), i16), shape(through.shape, through.dtype)]
    kernel = functools.partial(near_kernel, begin, end)
    return quick(kernel, "near_%d" % begin, [VMEM] * 4, out_shape)(part, norm, got, through)


def own_products(picks, embeddings, received, mine, other, through):
    total, dims = mine.shape
    out_shape = [shape((total, pack), f32), shape((8, pack), f32), shape(through.shape, through.dtype)]
    scratch = [pltpu.VMEM((pack, dims), bf16), pltpu.VMEM((pack, dims), bf16), pltpu.SemaphoreType.DMA((6,))]
    in_specs = [VMEM, ANY, ANY, VMEM, VMEM, VMEM]
    call = quick(own_kernel, "products_own", in_specs, out_shape, 46, scratch)
    return call(picks, embeddings, received, mine, other, through)


def finish_kernel(quality_ref, own_ref, norm_ref, g1, g2, inv_high, inv_low, out_ref, resid_ref, stage_ref, sent):
    total, width = own_ref.shape
    inverse_high, inverse_low = inv_high[...], inv_low[...]
    tile = width // 3
    copies = []
    for i in range(3):
        here = pl.ds(i * tile, tile)
        values, norm = own_ref[:, here], norm_ref[:1, here]
        for ref in (g1, g2):
            more, more_norm = decoded(ref, here, total)
            values, norm = values + more, norm + more_norm
        high = values.astype(bf16)
        low = (values - high.astype(f32)).astype(bf16)
        columns = jnp.dot(inverse_high, high, preferred_element_type=f32)
        columns += jnp.dot(inverse_high, low, preferred_element_type=f32)
        columns += jnp.dot(inverse_low, high, preferred_element_type=f32)
        score = quality_ref[here].reshape(1, tile)
        stage_ref[:, here] = columns * score
        copies.append(pltpu.make_async_copy(stage_ref.at[:, here], out_ref.at[:, here], sent.at[i]))
        copies[-1].start()
        left = norm + ridge_term - jnp.sum(columns * columns, axis=0, keepdims=True)
        resid_ref[here] = (score * score * left).reshape(tile)
    for copy in copies:
        copy.wait()


def finish(quality, own, norm, got, inverse):
    total, width = own.shape
    return pl.pallas_call(
        finish_kernel,
        in_specs=[VMEM] * 7,
        out_specs=[ANY, VMEM],
        out_shape=[shape((total, width), f32), shape((width,), f32)],
        scratch_shapes=[pltpu.VMEM((total, width), f32), pltpu.SemaphoreType.DMA((3,))],
        compiler_params=params(16),
        cost_estimate=cost(12 * total * total * width, 4 << 20),
        name="finish",
    )(quality, own, norm, *got, *inverse)


def along_y(k):
    return [(r, r ^ k) for r in range(Y * Z)]


def along_z(partner):
    return [(r, partner(r // Y) * Y + r % Y) for r in range(Y * Z)]


def along_x(k):
    return [(d, (d // 2 + k) % X * 2 + d % 2) for d in range(2 * X)]


swap = [(d, d ^ 1) for d in range(2 * X)]
both_ways = [(d, (d // 2 + (1 if d % 2 == 0 else -1)) % X * 2 + d % 2) for d in range(2 * X)]


def per_device(embeddings, quality, picked_rows):
    total = picked_rows.size
    with jax.named_scope("swap_rows"):
        received = lax.ppermute(embeddings, "dim", swap)

    with jax.named_scope("gather_picks"):
        parts = local_picks(picked_rows, embeddings)
        mine = parts[0]
        for k in (3, 2, 1):
            mine = mine + lax.ppermute(parts[k], "rows", along_y(k))
        staged = {}
        mine = mine + lax.ppermute(mine, "rows", along_z(lambda z: z ^ 1))
        arrived = lax.ppermute(mine, "rows", along_z(lambda z: z ^ 2))
        *staged[2], mine = stage(2, embeddings, received, mine)
        mine = mine + arrived
        arrived = lax.ppermute(mine, "rows", along_z(lambda z: z ^ 7))
        *staged[1], mine = stage(1, embeddings, received, mine)
        mine = mine + arrived
        groups = [mine] + [lax.ppermute(mine, "rows", along_y(k)) for k in range(1, Y)]
        *staged[3], mine = stage(3, embeddings, received, mine)
        groups[0] = mine
        pick_mine = in_order(groups)
        pick_other = lax.ppermute(pick_mine, "dim", swap)

    with jax.named_scope("sum_products"):
        to_next, to_last, token = far_products(staged[2], pick_mine, pick_other)
        from_last = lax.ppermute(to_next, "dim", along_x(1))
        from_next = lax.ppermute(to_last, "dim", along_x(3))
        full, half, keep = picks_gram(pick_mine, pick_other, token)
        gram_near = lax.ppermute(full, "dim", both_ways)
        gram_far = lax.ppermute(half, "dim", along_x(2))
        for_next, for_last, keep = both_products(staged[1], staged[3], pick_mine, pick_other, keep)
        onward, keep = near_block(0, cut, for_next, staged[1][2], from_last, keep)
        got_last = lax.ppermute(onward, "dim", along_x(1))
        onward, keep = near_block(cut, pack, for_last, staged[3][2], from_next, keep)
        got_next = lax.ppermute(onward, "dim", along_x(3))
    with jax.named_scope("sum_gram"):
        gram = jnp.concatenate([keep[:128] + gram_near[:128] + gram_far, keep[128:] + gram_near[128:]], axis=0)
        gram_other = lax.ppermute(gram, "dim", swap)
    own, norm, gram = own_products(picked_rows, embeddings, received, pick_mine, pick_other, gram)
    inverse = factor_inverse(gram, gram_other, total)
    columns, residual = finish(quality, own, norm, [got_last, got_next], inverse)
    return columns.T, residual


def solution(mesh):
    return jax.shard_map(
        per_device,
        mesh=mesh,
        in_specs=(P("rows", "dim"), P(("rows", "dim")), P()),
        out_specs=(P(("rows", "dim"), None), P(("rows", "dim"))),
        check_vma=False,
    )
```

```python
import functools

import jax
import jax.numpy as jnp
from jax import lax
from jax.experimental import pallas as pl
from jax.experimental.pallas import tpu as pltpu
from jax.sharding import PartitionSpec as P

ridge_term = 0.5
pack = 1152
Y, Z, X = 4, 8, 4
HIGHEST = lax.Precision.HIGHEST
NT = (((1,), (1,)), ((), ()))
TN = (((0,), (0,)), ((), ()))
f32, bf16, i32, i16 = jnp.float32, jnp.bfloat16, jnp.int32, jnp.int16
VMEM = pl.BlockSpec(memory_space=pltpu.VMEM)
ANY = pl.BlockSpec(memory_space=pl.ANY)
levels = 32767.0


def params(mib):
    return pltpu.CompilerParams(vmem_limit_bytes=mib << 20)


def cost(flops, nbytes):
    return pl.CostEstimate(flops=int(flops), bytes_accessed=int(nbytes), transcendentals=0)


def shape(dims, dtype):
    return jax.ShapeDtypeStruct(dims, dtype)


def as_column(row):
    n = row.shape[1]
    eye = lax.broadcasted_iota(i32, (n, n), 0) == lax.broadcasted_iota(i32, (n, n), 1)
    wide = jnp.broadcast_to(row.astype(f32), (n, n))
    return jnp.sum(jnp.where(eye, wide, 0.0), axis=1, keepdims=True).astype(i32)


def pick_kernel(picks_ref, e_ref, *rest):
    outs, (list_ref, tiles_ref, rows_ref, arrived) = rest[:Y], rest[Y:]
    rounds, count = picks_ref.shape
    total = rounds * count
    height = tiles_ref.shape[1]
    rows_here = e_ref.shape[0]
    row_start = lax.axis_index("rows") * rows_here
    held = jnp.int32(0)
    for p in range(total):
        local = picks_ref[p // count, p % count] - row_start
        list_ref[held] = local * 256 + p
        held = held + jnp.where((local >= 0) & (local < rows_here), 1, 0)

    def fetch(i):
        tile = pl.multiple_of(lax.div(list_ref[i], 256 * height) * height, height)
        return pltpu.make_async_copy(e_ref.at[pl.ds(tile, height), :], tiles_ref.at[i], arrived.at[i])

    def begin(i, carry):
        fetch(i).start()
        return carry

    def end(i, carry):
        fetch(i).wait()
        sub = lax.broadcasted_iota(i32, tiles_ref.shape[1:], 0)
        place, p = lax.div(list_ref[i], 256), lax.rem(list_ref[i], 256)
        one = jnp.where(sub == lax.rem(place, height), tiles_ref[i].astype(f32), 0.0)
        rows_ref[pl.ds(p, 1), :] = jnp.sum(one, axis=0, keepdims=True)
        return carry

    lax.fori_loop(0, held, begin, 0)
    rows_ref[...] = jnp.zeros_like(rows_ref)
    lax.fori_loop(0, held, end, 0)
    y = lax.rem(lax.axis_index("rows"), Y)
    group = total // Y
    for j in range(Y):
        g = lax.bitwise_xor(y, j)
        outs[j][...] = rows_ref[pl.ds(pl.multiple_of(g * group, 16), group), :].astype(bf16)


def local_picks(picks, embeddings):
    dims = embeddings.shape[1]
    total = picks.size
    return pl.pallas_call(
        pick_kernel,
        in_specs=[pl.BlockSpec(memory_space=pltpu.SMEM), ANY],
        out_specs=[VMEM] * Y,
        out_shape=[shape((total // Y, dims), bf16)] * Y,
        scratch_shapes=[
            pltpu.SMEM((256,), i32),
            pltpu.VMEM((total, 16, dims), bf16),
            pltpu.VMEM((total, dims), f32),
            pltpu.SemaphoreType.DMA((total,)),
        ],
        compiler_params=params(50),
        cost_estimate=cost(0, 10 << 20),
        name="local_picks",
    )(picks, embeddings)


def fetch_rows(hop, e_ref, r_ref, mine_ref, other_ref, arrived):
    d = lax.axis_index("dim")
    chip, core = lax.div(d, 2), lax.rem(d, 2)
    first = (lax.rem(chip + hop, X) * 2 + core) * pack
    tile = pack // 3
    copies = []
    for i in range(3):
        there, here = pl.ds(pl.multiple_of(first + i * tile, 128), tile), pl.ds(i * tile, tile)
        copies.append(
            (
                pltpu.make_async_copy(e_ref.at[there, :], mine_ref.at[here, :], arrived.at[2 * i]),
                pltpu.make_async_copy(r_ref.at[there, :], other_ref.at[here, :], arrived.at[2 * i + 1]),
            )
        )
    for pair in copies:
        for copy in pair:
            copy.start()
    return copies


def squared_norms(i, mine_ref, other_ref):
    tile = pack // 3
    squares = jnp.zeros((tile, 128), f32)
    for ref in (mine_ref, other_ref):
        for j in range(0, ref.shape[1], 128):
            part = ref[i * tile : (i + 1) * tile, j : j + 128].astype(f32)
            squares += part * part
    high = squares.astype(bf16)
    low = (squares - high.astype(f32)).astype(bf16)
    ones = jnp.ones((8, 128), bf16)
    norm = lax.dot_general(ones, high, NT, preferred_element_type=f32)
    return norm + lax.dot_general(ones, low, NT, preferred_element_type=f32)


def stage_kernel(hop, e_ref, r_ref, through_ref, mine_ref, other_ref, norm_ref, passed_ref, arrived):
    copies = fetch_rows(hop, e_ref, r_ref, mine_ref, other_ref, arrived)
    passed_ref[...] = through_ref[...]
    tile = pack // 3
    for i in range(3):
        for copy in copies[i]:
            copy.wait()
        norm_ref[:, i * tile : (i + 1) * tile] = squared_norms(i, mine_ref, other_ref)


def stage(hop, embeddings, received, through):
    dims = embeddings.shape[1]
    return pl.pallas_call(
        functools.partial(stage_kernel, hop),
        in_specs=[ANY, ANY, VMEM],
        out_specs=[VMEM] * 4,
        out_shape=[
            shape((pack, dims), bf16),
            shape((pack, dims), bf16),
            shape((8, pack), f32),
            shape(through.shape, through.dtype),
        ],
        scratch_shapes=[pltpu.SemaphoreType.DMA((6,))],
        compiler_params=params(50),
        cost_estimate=cost(0, 4 * pack * dims),
        name="stage_%d" % hop,
    )(embeddings, received, through)


def order_kernel(s0, s1, s2, s3, out_ref):
    y = lax.rem(lax.axis_index("rows"), Y)
    group = s0.shape[0]
    for j, ref in enumerate((s0, s1, s2, s3)):
        g = pl.multiple_of(lax.bitwise_xor(y, j) * group, 16)
        out_ref[pl.ds(g, group), :] = ref[...]


def in_order(groups):
    group, dims = groups[0].shape
    return pl.pallas_call(
        order_kernel,
        in_specs=[VMEM] * Y,
        out_specs=VMEM,
        out_shape=shape((group * Y, dims), bf16),
        compiler_params=params(16),
        cost_estimate=cost(0, 4 * Y * group * dims),
        name="order",
    )(*groups)


def gram_kernel(mine_ref, other_ref, token_ref, full_ref, half_ref, keep_ref):
    mine, other = mine_ref[...], other_ref[...]
    gram = lax.dot_general(mine, mine, NT, preferred_element_type=f32)
    gram += lax.dot_general(other, other, NT, preferred_element_type=f32)
    core = lax.rem(lax.axis_index("dim"), 2)
    top = gram[:128, :128]
    corner = jnp.concatenate([gram[128:, 128:], jnp.zeros((64, 64), f32)], axis=1)
    low = jnp.concatenate([gram[128:, :128], corner], axis=0)
    a, b = jnp.where(core == 0, top, low), jnp.where(core == 0, low, top)
    half_ref[...] = a
    full_ref[:128, :], full_ref[128:, :] = a, b
    keep_ref[:128, :], keep_ref[128:, :] = jnp.where(core == 0, a, 0.0), jnp.where(core == 0, b, 0.0)


def picks_gram(mine, other, token):
    total, dims = mine.shape
    return pl.pallas_call(
        gram_kernel,
        in_specs=[VMEM] * 3,
        out_specs=[VMEM] * 3,
        out_shape=[shape((256, 128), f32), shape((128, 128), f32), shape((256, 128), f32)],
        compiler_params=params(16),
        cost_estimate=cost(4 * total * total * dims, 4 * total * dims),
        name="gram",
    )(mine, other, token)


panel, together = 64, 8


def factor_kernel(sum_ref, swapped_ref, high_ref, low_ref, m_ref):
    n = high_ref.shape[0]
    core = lax.rem(lax.axis_index("dim"), 2)
    a = sum_ref[:128, :] + swapped_ref[128:, :]
    b = sum_ref[128:, :] + swapped_ref[:128, :]
    first, last = jnp.where(core == 0, a, b), jnp.where(core == 0, b, a)
    width = m_ref.shape[1]
    sub = lax.broadcasted_iota(i32, (n, width - 128), 0)
    lane = lax.broadcasted_iota(i32, (n, width - 128), 1) + 128
    m_ref[:, 128:] = jnp.where(lane - n == sub, 1.0, 0.0)
    diag = lax.broadcasted_iota(i32, (128, 128), 0) == lax.broadcasted_iota(i32, (128, 128), 1)
    ridge = jnp.where(diag, ridge_term, 0.0)
    m_ref[:128, :128] = first + ridge
    m_ref[128:, :128] = last[:64, :]
    m_ref[128:, 128:n] = last[64:, :64] + ridge[:64, :64]
    m_ref[:128, 128:n] = last[:64, :].T
    below = lax.broadcasted_iota(i32, (panel, 128), 0)
    at = lax.broadcasted_iota(i32, (panel, 128), 1) - below
    for low in range(0, n, panel):
        left = low // 128 * 128
        off = low - left
        tiles = [m_ref[low : low + panel, j : j + 128] for j in range(left, width, 128)]
        done = []
        for g in range(0, panel, together):
            height = panel - g
            cols = [
                jnp.broadcast_to(tiles[0][:, off + g + i : off + g + i + 1], (height, 128)) for i in range(together)
            ]
            heads = [[t[i : i + 1, :] for t in tiles] for i in range(together)]
            for i in range(together):
                factors = jnp.where(below[:height] > i, cols[i] * (1.0 / cols[i][i : i + 1, :]), 0.0)
                for j in range(i + 1, together):
                    cols[j] = cols[j] - factors * cols[j][i : i + 1, :]
                    by = factors[j : j + 1, :]
                    heads[j] = [x - by * y for x, y in zip(heads[j], heads[i])]
                tiles = [t - factors * y for t, y in zip(tiles, heads[i])]
            done.append([t[:together, :] for t in tiles])
            tiles = [t[together:, :] for t in tiles]
        tiles = [jnp.concatenate(pieces, axis=0) for pieces in zip(*done)]
        pivots = jnp.sum(jnp.where(at == off, tiles[0], 0.0), axis=1, keepdims=True)
        rows = jnp.concatenate(tiles, axis=1) * (1.0 / jnp.sqrt(pivots))
        inverse = rows[:, n - left :]
        high = inverse.astype(bf16)
        high_ref[low : low + panel, :] = high
        low_ref[low : low + panel, :] = (inverse - high.astype(f32)).astype(bf16)
        if low + panel < n:
            update = lax.dot_general(rows[:, : n - left], rows, TN, precision=HIGHEST, preferred_element_type=f32)
            m_ref[low + panel :, left:] -= update[low + panel - left :, :]


def factor_inverse(total, swapped, n):
    return pl.pallas_call(
        factor_kernel,
        in_specs=[VMEM] * 2,
        out_specs=[VMEM] * 2,
        out_shape=[shape((n, n), bf16)] * 2,
        scratch_shapes=[pltpu.VMEM((n, 2 * n), f32)],
        compiler_params=params(16),
        cost_estimate=cost(1e6, 1 << 16),
        name="factor",
    )(total, swapped)


def split(value):
    scaled = value * 8.0
    high = jnp.floor(scaled)
    return high, jnp.floor((scaled - high) * 32768.0)


def join(high, low):
    return (high + low * (1.0 / 32768.0)) * (1.0 / 8.0)


def block_products(at, e_ref, r_ref, mine_ref, other_ref):
    part = lax.dot_general(mine_ref[...], e_ref[at, :], NT, preferred_element_type=f32)
    return part + lax.dot_general(other_ref[...], r_ref[at, :], NT, preferred_element_type=f32)


def coded(part, norm):
    norm_high, norm_low = split(norm)
    top_high, top_low = split(jnp.max(jnp.abs(part), axis=0, keepdims=True))
    scale = join(top_high, top_low + 1.0)
    whole = jnp.floor(part * (levels / scale) + 0.5)
    row = lax.broadcasted_iota(i32, (8, part.shape[1]), 0)
    extra = jnp.where(row == 0, norm_high, jnp.where(row == 1, norm_low, jnp.where(row == 2, top_high, top_low)))
    return jnp.concatenate([whole, extra], axis=0).astype(i32).astype(i16)


def decoded(ref, at, total):
    got = ref[:, at].astype(i32).astype(f32)
    scale = join(got[total + 2 : total + 3], got[total + 3 : total + 4] + 1.0)
    norm = join(got[total : total + 1], got[total + 1 : total + 2] + 0.5)
    return got[:total] * (scale * (1.0 / levels)), norm


cut = 640
spans = ((0, 384), (384, 256), (640, 512))


def far_kernel(e_ref, r_ref, norm_ref, mine_ref, other_ref, low_ref, high_ref, token_ref):
    for low, width in spans:
        at = pl.ds(low, width)
        part = block_products(at, e_ref, r_ref, mine_ref, other_ref)
        out = coded(part, norm_ref[:1, at])
        if low < cut:
            low_ref[:, at] = out
        else:
            high_ref[:, low - cut : low - cut + width] = out
    token_ref[...] = jnp.zeros_like(token_ref)


def both_kernel(e_next, r_next, e_last, r_last, mine_ref, other_ref, through_ref, next_ref, last_ref, passed_ref):
    passed_ref[...] = through_ref[...]
    for low, width in spans:
        at = pl.ds(low, width)
        next_ref[:, at] = block_products(at, e_next, r_next, mine_ref, other_ref)
        last_ref[:, at] = block_products(at, e_last, r_last, mine_ref, other_ref)


def near_kernel(begin, end, part_ref, norm_ref, got_ref, through_ref, out_ref, passed_ref):
    total = part_ref.shape[0]
    passed_ref[...] = through_ref[...]
    for low, width in spans:
        at = pl.ds(low, width)
        part, norm = part_ref[:, at], norm_ref[:1, at]
        if begin <= low < end:
            more, more_norm = decoded(got_ref, pl.ds(low - begin, width), total)
            part, norm = part + more, norm + more_norm
        out_ref[:, at] = coded(part, norm)


def own_kernel(
    picks_ref, e_ref, r_ref, mine_ref, other_ref, through_ref, out_ref, norm_ref, passed_ref, e_here, r_here, arrived
):
    copies = fetch_rows(0, e_ref, r_ref, e_here, r_here, arrived)
    passed_ref[...] = through_ref[...]
    rounds, count = picks_ref.shape
    first_row = (lax.axis_index("rows") * (2 * X) + lax.axis_index("dim")) * pack
    chosen = jnp.concatenate([as_column(picks_ref[r : r + 1, :]) for r in range(rounds)], axis=0) - first_row
    tile = pack // 3
    for i in range(3):
        for copy in copies[i]:
            copy.wait()
        at = slice(i * tile, (i + 1) * tile)
        norm_ref[:, at] = squared_norms(i, e_here, r_here)
        part = block_products(pl.ds(i * tile, tile), e_here, r_here, mine_ref, other_ref)
        lane = lax.broadcasted_iota(i32, part.shape, 1) + i * tile
        out_ref[:, at] = jnp.where(chosen == lane, part + ridge_term, part)


def quick(kernel, name, in_specs, out_shape, mib=16, scratch=(), flops=1e6):
    return pl.pallas_call(
        kernel,
        in_specs=in_specs,
        out_specs=[VMEM] * len(out_shape),
        out_shape=out_shape,
        scratch_shapes=scratch,
        compiler_params=params(mib),
        cost_estimate=cost(flops, 1 << 16),
        name=name,
    )


def far_products(staged, mine, other):
    total = mine.shape[0]
    out_shape = [shape((total + 8, cut), i16), shape((total + 8, pack - cut), i16), shape((8, 128), f32)]
    return quick(far_kernel, "products_far", [VMEM] * 5, out_shape)(*staged, mine, other)


def both_products(following, last, mine, other, through):
    total = mine.shape[0]
    out_shape = [shape((total, pack), f32)] * 2 + [shape(through.shape, through.dtype)]
    return quick(both_kernel, "products_both", [VMEM] * 7, out_shape)(*following[:2], *last[:2], mine, other, through)


def near_block(begin, end, part, norm, got, through):
    out_shape = [shape((part.shape[0] + 8, pack), i16), shape(through.shape, through.dtype)]
    kernel = functools.partial(near_kernel, begin, end)
    return quick(kernel, "near_%d" % begin, [VMEM] * 4, out_shape)(part, norm, got, through)


def own_products(picks, embeddings, received, mine, other, through):
    total, dims = mine.shape
    out_shape = [shape((total, pack), f32), shape((8, pack), f32), shape(through.shape, through.dtype)]
    scratch = [pltpu.VMEM((pack, dims), bf16), pltpu.VMEM((pack, dims), bf16), pltpu.SemaphoreType.DMA((6,))]
    in_specs = [VMEM, ANY, ANY, VMEM, VMEM, VMEM]
    call = quick(own_kernel, "products_own", in_specs, out_shape, 46, scratch)
    return call(picks, embeddings, received, mine, other, through)


def finish_kernel(quality_ref, own_ref, norm_ref, g1, g2, inv_high, inv_low, out_ref, resid_ref, stage_ref, sent):
    total, width = own_ref.shape
    inverse_high, inverse_low = inv_high[...], inv_low[...]
    copies = []
    for i, (start, tile) in enumerate(((0, 512), (512, 384), (896, 256))):
        here = pl.ds(start, tile)
        values, norm = own_ref[:, here], norm_ref[:1, here]
        for ref in (g1, g2):
            more, more_norm = decoded(ref, here, total)
            values, norm = values + more, norm + more_norm
        high = values.astype(bf16)
        low = (values - high.astype(f32)).astype(bf16)
        columns = jnp.dot(inverse_high, high, preferred_element_type=f32)
        columns += jnp.dot(inverse_high, low, preferred_element_type=f32)
        columns += jnp.dot(inverse_low, high, preferred_element_type=f32)
        score = quality_ref[here].reshape(1, tile)
        stage_ref[:, here] = columns * score
        copies.append(pltpu.make_async_copy(stage_ref.at[:, here], out_ref.at[:, here], sent.at[i]))
        copies[-1].start()
        left = norm + ridge_term - jnp.sum(columns * columns, axis=0, keepdims=True)
        resid_ref[here] = (score * score * left).reshape(tile)
    for copy in copies:
        copy.wait()


def finish(quality, own, norm, got, inverse):
    total, width = own.shape
    return pl.pallas_call(
        finish_kernel,
        in_specs=[VMEM] * 7,
        out_specs=[ANY, VMEM],
        out_shape=[shape((total, width), f32), shape((width,), f32)],
        scratch_shapes=[pltpu.VMEM((total, width), f32), pltpu.SemaphoreType.DMA((3,))],
        compiler_params=params(16),
        cost_estimate=cost(12 * total * total * width, 4 << 20),
        name="finish",
    )(quality, own, norm, *got, *inverse)


def along_y(k):
    return [(r, r ^ k) for r in range(Y * Z)]


def along_z(partner):
    return [(r, partner(r // Y) * Y + r % Y) for r in range(Y * Z)]


def along_x(k):
    return [(d, (d // 2 + k) % X * 2 + d % 2) for d in range(2 * X)]


swap = [(d, d ^ 1) for d in range(2 * X)]
both_ways = [(d, (d // 2 + (1 if d % 2 == 0 else -1)) % X * 2 + d % 2) for d in range(2 * X)]


def per_device(embeddings, quality, picked_rows):
    total = picked_rows.size
    with jax.named_scope("swap_rows"):
        received = lax.ppermute(embeddings, "dim", swap)

    with jax.named_scope("gather_picks"):
        parts = local_picks(picked_rows, embeddings)
        mine = parts[0]
        for k in (3, 2, 1):
            mine = mine + lax.ppermute(parts[k], "rows", along_y(k))
        staged = {}
        mine = mine + lax.ppermute(mine, "rows", along_z(lambda z: z ^ 1))
        arrived = lax.ppermute(mine, "rows", along_z(lambda z: z ^ 2))
        *staged[2], mine = stage(2, embeddings, received, mine)
        mine = mine + arrived
        arrived = lax.ppermute(mine, "rows", along_z(lambda z: z ^ 7))
        *staged[1], mine = stage(1, embeddings, received, mine)
        mine = mine + arrived
        groups = [mine] + [lax.ppermute(mine, "rows", along_y(k)) for k in range(1, Y)]
        *staged[3], mine = stage(3, embeddings, received, mine)
        groups[0] = mine
        pick_mine = in_order(groups)
        pick_other = lax.ppermute(pick_mine, "dim", swap)

    with jax.named_scope("sum_products"):
        to_next, to_last, token = far_products(staged[2], pick_mine, pick_other)
        from_last = lax.ppermute(to_next, "dim", along_x(1))
        from_next = lax.ppermute(to_last, "dim", along_x(3))
        full, half, keep = picks_gram(pick_mine, pick_other, token)
        gram_near = lax.ppermute(full, "dim", both_ways)
        gram_far = lax.ppermute(half, "dim", along_x(2))
        for_next, for_last, keep = both_products(staged[1], staged[3], pick_mine, pick_other, keep)
        onward, keep = near_block(0, cut, for_next, staged[1][2], from_last, keep)
        got_last = lax.ppermute(onward, "dim", along_x(1))
        onward, keep = near_block(cut, pack, for_last, staged[3][2], from_next, keep)
        got_next = lax.ppermute(onward, "dim", along_x(3))
    with jax.named_scope("sum_gram"):
        gram = jnp.concatenate([keep[:128] + gram_near[:128] + gram_far, keep[128:] + gram_near[128:]], axis=0)
        gram_other = lax.ppermute(gram, "dim", swap)
    own, norm, gram = own_products(picked_rows, embeddings, received, pick_mine, pick_other, gram)
    inverse = factor_inverse(gram, gram_other, total)
    columns, residual = finish(quality, own, norm, [got_last, got_next], inverse)
    return columns.T, residual


def solution(mesh):
    return jax.shard_map(
        per_device,
        mesh=mesh,
        in_specs=(P("rows", "dim"), P(("rows", "dim")), P()),
        out_specs=(P(("rows", "dim"), None), P(("rows", "dim"))),
        check_vma=False,
    )
```
